512 devices in a mesh: wide: 32 (over y, x_hi, core), blk: 16 (over x_lo, z).
Axes of the slice: x: 4 (x_hi: 2, x_lo: 2; x = x_hi * 2 + x_lo), y: 8, z: 8, core: 2. Of those that a mesh axis runs over, the one named last changes fastest.
Arguments:
- audio: bfloat16 [65536, 1024], P(('wide', 'blk')), may hold values from -1 to 1
- video: bfloat16 [65536, 1024], P(('wide', 'blk')), may hold values from -1 to 1
- owner: int32 [65536, 1], P(('wide', 'blk')), may hold values from 0 to 31; in each aligned block of 128 rows (0 to 127, 128 to 255, ...) at most 8 rows name the same one
- clip_feats: bfloat16 [131072, 1024], P(('wide', 'blk')), may hold values from -48 to 48
- lengths: int32 [131072], P(('wide', 'blk')), may hold values from 1 to 16
- proj_weight: bfloat16 [1024, 1024], replicated, may hold values from -0.1875 to 0.1875
Outputs:
- audio_grad: bfloat16 [65536, 1024], P(('wide', 'blk'))
- feats_grad: bfloat16 [131072, 1024], P(('wide', 'blk'))
- weight_grad: float32 [1024, 1024], P('wide')
The draws below stay inside these ranges and needn't reach their ends.
Inputs may be any that keep to these rules, and one draw needn't show every extreme that they name: Among the 128 rows of one device, no owner is named more than 8 times, a bound that some block reaches.
All inputs are finite; a program needn't handle non-finite values.
Results may differ from the reference program's by a relative error of at most 0.02.
Values may be sent and summed in bfloat16 or wider, within the bound.
No kernel may reach another device: no remote copies, remote signals or barrier semaphores. Data moves between devices by JAX's collectives and lax.ppermute only.
A program may use at most 64 MiB of HBM per device.

```python
import math
from functools import partial
import jax
import jax.numpy as jnp
import numpy as np
from jax import lax

EMBED = 1024
CLIPS_DEV = 128
CAP = 8
ROWS = 65536
SLOTS_ALL = 131072
N_WIDE = 32
N_BLK = 16


def plant(entries, key, low, largest):
    shape = entries.shape
    index_at = [jax.random.randint(jax.random.fold_in(key, axis), (), 0, shape[axis]) for axis in range(len(shape))]
    entries = entries.at[tuple(index_at)].set(low)
    longest = shape.index(max(shape))
    index_at[longest] = (index_at[longest] + 1) % shape[longest]
    return entries.at[tuple(index_at)].set(largest)


def raised(drawn, rng, source, target, blocks, factor):
    owner, partner = [(jnp.arange(drawn.shape[dim]) // (drawn.shape[dim] // blocks)).reshape([-1 if axis == dim else 1 for axis in range(drawn.ndim)]) for dim in (source, target)]
    chosen = jax.random.permutation(rng, blocks)[partner]
    strong = (owner == chosen) | (owner == (partner + blocks // 2) % blocks)
    return jnp.where(strong, factor * drawn, drawn)


def level_of(stream_key, extent, pieces, least, high):
    factor_of = 1.0
    for axis_at, parts in pieces:
        heights = jax.random.uniform(jax.random.fold_in(jax.random.fold_in(stream_key, 6), axis_at), (parts,), jnp.float32, least / len(pieces), high / len(pieces))
        factor_of = factor_of * jnp.repeat(jnp.exp(heights), extent[axis_at] // parts).reshape((-1,) + (1,) * (len(extent) - 1 - axis_at))
    return factor_of


def routed_block(stream_key, own, number, rows, amount, top, bound, lean):
    sequence = jax.random.permutation(stream_key, amount)
    packed, ordinary = portions_of(amount, rows * top, bound, lean, True), portions_of(amount, rows * top, bound, lean, False)
    places = jnp.arange(amount)

    def named(sizes, turn):
        used = int((sizes > 0).sum())
        fixed = max(1, used // 4)
        passed = fixed + (places - fixed + turn * (used - fixed)) % max(1, amount - fixed)
        return jnp.zeros((amount,), jnp.int32).at[sequence[jnp.where(places < fixed, places, passed)]].set(jnp.asarray(sizes, jnp.int32))

    sizes = jnp.where(number % 4 == 0, named(packed, number // 4), named(ordinary, number - number // 4 - 1))
    mixed = jax.random.permutation(jax.random.fold_in(own, 3), amount)
    source_of, sink = mixed[0:amount // 2 * 2:2], mixed[1:amount // 2 * 2:2]
    room = jnp.minimum(sizes[source_of] - 1, bound - sizes[sink]) // 2
    room = jnp.where((source_of == sequence[0]) | (sink == sequence[0]) | (sizes[sink] == 0), 0, jnp.maximum(room, 0))
    passed = jax.random.randint(jax.random.fold_in(own, 4), (amount // 2,), 0, 1 << 20) % (room + 1)
    sizes = sizes.at[source_of].add(-passed).at[sink].add(passed)
    items = jnp.searchsorted(jnp.cumsum(sizes), jnp.arange(rows * top), side="right").astype(jnp.int32)
    grid = items.reshape(top, rows).T
    grid = grid[jax.random.permutation(jax.random.fold_in(own, 1), rows)]
    turn = jax.random.randint(jax.random.fold_in(own, 2), (rows, 1), 0, top)
    return jnp.take_along_axis(grid, (jnp.arange(top)[None, :] + turn) % top, axis=1)


def portions_of(amount, total, bound, lean, full):
    weights = [(1 << 20) // math.isqrt(rank ** lean) + 1 for rank in range(1, amount + 1)]
    largest = bound if full else min(bound, max(-(-total // amount), total * weights[0] // sum(weights)))
    least = 1 if total - largest >= amount - 1 else 0
    counts, rest = [largest] + [least] * (amount - 1), total - largest - least * (amount - 1)
    while rest > 0:
        free = [i for i in range(1, amount) if counts[i] < largest] or [i for i in range(1, amount) if counts[i] < bound]
        mass, budget = sum([weights[i] for i in free]), rest
        for i in free:
            more = min(bound - counts[i], max(1, budget * weights[i] // mass), rest)
            counts[i] = counts[i] + more
            rest = rest - more
    return np.array(counts)


def scatter_about(stream_key, shape, width, bound, shards=(), kind=jnp.bfloat16):
    entries = jax.random.normal(stream_key, shape, jnp.float32) * width
    if len(shards) > 0:
        entries = level_of(stream_key, shape, shards, -0.22, 0.18) * entries
    return jnp.clip(entries, min=-bound, max=bound).astype(kind)


def bell_draw_with(rng, shape, scale, limit, split, heavy, held_as=jnp.bfloat16):
    drawn = scale * jax.random.normal(rng, shape, jnp.float32)
    if split:
        drawn = drawn * level_of(rng, shape, split, -0.22, 0.18)
    return jnp.clip(raised(drawn, jax.random.fold_in(rng, 3), *heavy), -limit, limit).astype(held_as)


def setup_inputs(seed: int = 0) -> dict:
    streams_of = jax.random.split(jax.random.key(seed), 7)
    audio = scatter_about(streams_of[0], (ROWS, EMBED), 0.177, 1.0, ((0, 512),))
    video = scatter_about(streams_of[1], (ROWS, EMBED), 0.177, 1.0, ((0, 512),))
    owner_keys = jax.random.split(jax.random.fold_in(streams_of[2], 1), ROWS // CLIPS_DEV)
    owner_turns = jax.random.permutation(jax.random.fold_in(streams_of[2], 3), ROWS // CLIPS_DEV)
    owner = jax.vmap(lambda own, number: routed_block(jax.random.fold_in(streams_of[2], 2), own, number, CLIPS_DEV, N_WIDE, 1, CAP, 2))(owner_keys, owner_turns).reshape((ROWS, 1))
    clip_feats = bell_draw_with(streams_of[3], (SLOTS_ALL, EMBED), 2.0, 48.0, ((0, 512),), (0, 1, 512, 6.0))
    lengths = plant(jax.random.randint(streams_of[4], (SLOTS_ALL,), 1, 17), jax.random.fold_in(streams_of[4], 1), 1, 16).astype(jnp.int32)
    proj_weight = scatter_about(streams_of[5], (EMBED, EMBED), EMBED ** -0.5, 0.1875)
    return dict(audio=audio, video=video, owner=owner, clip_feats=clip_feats, lengths=lengths, proj_weight=proj_weight)


def group_grads(group_pair):
    audio_g, video_g = group_pair
    scores = jnp.dot(audio_g, video_g.T, preferred_element_type=jnp.float32)
    pair_count = audio_g.shape[0]
    labels = (jnp.arange(pair_count, dtype=jnp.int32)[:, None] == jnp.arange(pair_count, dtype=jnp.int32)[None, :]).astype(jnp.float32)
    coeffs = (4.0 / N_BLK * (jax.nn.sigmoid(4.0 * scores - 2.0) - labels)).astype(jnp.bfloat16)
    audio_part = jnp.dot(coeffs, video_g, preferred_element_type=jnp.float32).astype(jnp.bfloat16)
    video_part = jnp.dot(coeffs.T, audio_g, preferred_element_type=jnp.float32).astype(jnp.bfloat16)
    return (audio_part, video_part)

def reference(audio, video, owner, clip_feats, lengths, proj_weight):
    audio_groups = audio.reshape(N_WIDE, N_BLK * CLIPS_DEV, EMBED)
    video_groups = video.reshape(N_WIDE, N_BLK * CLIPS_DEV, EMBED)
    audio_grad, video_grad = lax.map(group_grads, (audio_groups, video_groups))
    audio_grad = audio_grad.reshape(ROWS, EMBED)
    owner_peer = owner.reshape(N_WIDE, N_BLK, CLIPS_DEV).astype(jnp.int32)
    onehot = (owner_peer[..., None] == jnp.arange(N_WIDE, dtype=jnp.int32)[None, None, None, :]).astype(jnp.int32)
    before = (jnp.cumsum(onehot, axis=2).astype(jnp.int32) - onehot) * onehot
    slot_rank = lax.optimization_barrier(jnp.sum(before, axis=3)).astype(jnp.int32)
    source = jnp.arange(N_WIDE, dtype=jnp.int32).reshape(N_WIDE, 1, 1)
    group_pos = jnp.arange(N_BLK, dtype=jnp.int32).reshape(1, N_BLK, 1)
    target = (((owner_peer * N_BLK + group_pos) * N_WIDE + source) * CAP + slot_rank).astype(jnp.int32)
    received = jnp.zeros((SLOTS_ALL, EMBED), jnp.bfloat16)
    received = received.at[target.reshape(-1)].set(video_grad.reshape(ROWS, EMBED))
    length_scale = lax.rsqrt(lengths.astype(jnp.float32))[:, None]
    pooled = (clip_feats.astype(jnp.float32) * length_scale).astype(jnp.bfloat16)
    preact = jnp.dot(pooled, proj_weight, preferred_element_type=jnp.float32)
    _, pullback = jax.vjp(partial(jax.nn.gelu, approximate=False), preact)
    pre_grad = pullback(received.astype(jnp.float32))[0].astype(jnp.bfloat16)
    feats_grad = (jnp.dot(pre_grad, proj_weight.T, preferred_element_type=jnp.float32) * length_scale).astype(jnp.bfloat16)
    weight_grad = jnp.dot(pooled.T, pre_grad, preferred_element_type=jnp.float32)
    return (audio_grad, feats_grad, weight_grad)
```

```python
import jax
import jax.numpy as jnp
from jax import lax
from jax.sharding import Mesh
from jax.sharding import PartitionSpec as P

AXES = ("wide_y", "wide_x", "wide_c", "blk_x", "blk_z")
WIDE = ("wide_y", "wide_x", "wide_c")
BLK = ("blk_x", "blk_z")
BF16 = jnp.bfloat16
F32 = jnp.float32


def swapped(array, axis):
    return lax.ppermute(array, axis, [(0, 1), (1, 0)])


def rows_dot(matrix_a, matrix_b):
    return lax.dot_general(
        matrix_a, matrix_b, (((1,), (1,)), ((), ())), preferred_element_type=F32
    )


def cols_dot(matrix_a, matrix_b):
    return lax.dot_general(
        matrix_a, matrix_b, (((0,), (0,)), ((), ())), preferred_element_type=F32
    )


def plain_dot(matrix_a, matrix_b):
    return jnp.dot(matrix_a, matrix_b, preferred_element_type=F32)


def gelu_slope(v):
    cdf = 0.5 * (1.0 + lax.erf(v * 0.7071067811865476))
    return cdf + v * (0.3989422804014327 * jnp.exp(-0.5 * v * v))


def pair_coeffs(scores, labels, factor):
    return (factor * (jax.nn.sigmoid(4.0 * scores - 2.0) - labels)).astype(BF16)


def placing_of(owner, slot_count, capacity):
    count = owner.shape[0]
    ids = jnp.arange(count, dtype=jnp.int32)
    peer = owner[:, 0]
    before = (peer[:, None] == peer[None, :]) & (ids[:, None] < ids[None, :])
    target = peer * capacity + jnp.sum(before.astype(jnp.int32), axis=0)
    return (jnp.arange(slot_count, dtype=jnp.int32)[:, None] == target[None, :]).astype(BF16)


def picking_of(core, feature_count):
    half = feature_count // 2
    ny, nx = lax.axis_size("wide_y"), lax.axis_size("wide_x")
    bx, bz = lax.axis_size("blk_x"), lax.axis_size("blk_z")
    share = half // (ny * nx * bx)
    place = jnp.arange(half, dtype=jnp.int32)
    within, rest = place % share, place // share
    y, rest = rest % ny, rest // ny
    x_blk, x_wide = rest % bx, rest // bx
    feature = (((y * nx + x_wide) * 2 + core) * bx + x_blk) * share + within
    return (jnp.arange(feature_count, dtype=jnp.int32)[:, None] == feature[None, :]).astype(BF16)


def shards(audio, video, owner, clip_feats, lengths, proj_weight):
    clips, features = audio.shape
    blocks = lax.axis_size(BLK)
    factor = 4.0 / blocks
    z, core = lax.axis_index("blk_z"), lax.axis_index("wide_c")
    nz = lax.axis_size("blk_z")

    audio_line = lax.all_gather(audio, "blk_z", axis=0, tiled=True)
    video_line = lax.all_gather(video, "blk_z", axis=0, tiled=True)

    peers = lax.axis_size(WIDE)
    slots = clip_feats.shape[0]
    capacity = slots // peers
    length_scale = lax.rsqrt(lengths.astype(F32))[:, None]
    pooled = (clip_feats.astype(F32) * length_scale).astype(BF16)
    pooled_slots = lax.all_to_all(
        pooled.reshape(peers, capacity, features), WIDE, 0, 0, tiled=True
    ).reshape(slots, features)
    both = swapped(jnp.concatenate([video, audio]), "blk_x")
    video_pair = jnp.concatenate([video, both[:clips]])
    audio_pair = jnp.concatenate([audio, both[clips:]])
    slope_own = gelu_slope(plain_dot(pooled, proj_weight))

    placing = placing_of(owner, slots, capacity)
    clip_rows = cols_dot(placing, pooled_slots).astype(BF16)
    row_pair = jnp.concatenate([clip_rows, swapped(clip_rows, "blk_x")])
    slope_pair = gelu_slope(plain_dot(row_pair, proj_weight))
    picked = plain_dot(row_pair, picking_of(core, features)).astype(BF16)
    other = plain_dot(row_pair, picking_of(1 - core, features)).astype(BF16)
    picked = jnp.concatenate([picked, swapped(other, "wide_c")])

    row_ids = jnp.arange(nz * clips, dtype=jnp.int32)[:, None]
    col_ids = jnp.arange(2 * clips, dtype=jnp.int32)[None, :]
    labels = ((row_ids == z * clips + col_ids) & (col_ids < clips)).astype(F32)
    coeffs = pair_coeffs(rows_dot(audio_line, video_pair), labels, factor)
    video_part = cols_dot(coeffs, audio_line)

    pre_part = (video_part * slope_pair).astype(BF16)
    pre_both = jnp.concatenate([pre_part, swapped(pre_part, "wide_c")])
    weight_part = cols_dot(picked, pre_both).astype(BF16)
    nx = lax.axis_size(("wide_x", "blk_x"))
    ny = lax.axis_size("wide_y")
    pieces = lax.all_to_all(
        weight_part.reshape(nx, -1, features), ("wide_x", "blk_x"), 0, 0, tiled=True
    )
    summed = jnp.sum(pieces.astype(F32), axis=0).astype(BF16)
    rows, cols = summed.shape[0] // ny, features // nz
    summed = summed.reshape(ny, rows, nz, cols).transpose(0, 2, 1, 3).reshape(ny * nz, rows, cols)
    pieces = lax.all_to_all(summed, ("wide_y", "blk_z"), 0, 0, tiled=True)
    total = jnp.sum(pieces.astype(F32), axis=0).astype(BF16)
    gathered = lax.all_to_all(
        jnp.broadcast_to(total[None], (blocks, rows, cols)), BLK, 0, 0, tiled=True
    )
    weight_grad = (
        gathered.reshape(-1, nz, rows, cols).transpose(0, 2, 1, 3).reshape(-1, features).astype(F32)
    )

    arrived = swapped(video_part[clips:].astype(BF16), "blk_x")
    video_grad = (video_part[:clips] + arrived.astype(F32)).astype(BF16)
    packed = plain_dot(placing, video_grad).astype(BF16)
    received = lax.all_to_all(
        packed.reshape(peers, capacity, features), WIDE, 0, 0, tiled=True
    ).reshape(slots, features)
    pre_grad = (received.astype(F32) * slope_own).astype(BF16)
    feats_grad = (rows_dot(pre_grad, proj_weight) * length_scale).astype(BF16)

    coeffs = pair_coeffs(rows_dot(audio_pair, video_line), labels.T, factor)
    audio_part = plain_dot(coeffs, video_line)
    arrived = swapped(audio_part[clips:].astype(BF16), "blk_x")
    audio_grad = (audio_part[:clips] + arrived.astype(F32)).astype(BF16)
    return (audio_grad, feats_grad, weight_grad)


def solution(mesh):
    finer = Mesh(mesh.devices.reshape(8, 2, 2, 2, 8), AXES)
    rows = P(AXES, None)
    return jax.shard_map(
        shards,
        mesh=finer,
        in_specs=(rows, rows, rows, rows, P(AXES), P()),
        out_specs=(rows, rows, P(WIDE, None)),
        check_vma=False,
    )
```

```python
import jax
import jax.numpy as jnp
from jax import lax
from jax.sharding import Mesh
from jax.sharding import PartitionSpec as P

AXES = ("wide_y", "wide_x", "wide_c", "blk_x", "blk_z")
WIDE = ("wide_y", "wide_x", "wide_c")
BLK = ("blk_x", "blk_z")
BF16 = jnp.bfloat16
F32 = jnp.float32


def swapped(array, axis):
    return lax.ppermute(array, axis, [(0, 1), (1, 0)])


def rows_dot(matrix_a, matrix_b):
    return lax.dot_general(
        matrix_a, matrix_b, (((1,), (1,)), ((), ())), preferred_element_type=F32
    )


def cols_dot(matrix_a, matrix_b):
    return lax.dot_general(
        matrix_a, matrix_b, (((0,), (0,)), ((), ())), preferred_element_type=F32
    )


def plain_dot(matrix_a, matrix_b):
    return jnp.dot(matrix_a, matrix_b, preferred_element_type=F32)


def gelu_slope(v):
    cdf = 0.5 * (1.0 + lax.erf(v * 0.7071067811865476))
    return cdf + v * (0.3989422804014327 * jnp.exp(-0.5 * v * v))


def pair_coeffs(scores, labels, factor):
    return (factor * (jax.nn.sigmoid(4.0 * scores - 2.0) - labels)).astype(BF16)


def placing_of(owner, slot_count, capacity):
    count = owner.shape[0]
    ids = jnp.arange(count, dtype=jnp.int32)
    peer = owner[:, 0]
    before = (peer[:, None] == peer[None, :]) & (ids[:, None] < ids[None, :])
    target = peer * capacity + jnp.sum(before.astype(jnp.int32), axis=0)
    return (jnp.arange(slot_count, dtype=jnp.int32)[:, None] == target[None, :]).astype(BF16)


def picking_of(core, feature_count):
    half = feature_count // 2
    ny, nx = lax.axis_size("wide_y"), lax.axis_size("wide_x")
    bx = lax.axis_size("blk_x")
    share = half // (ny * nx * bx)
    place = jnp.arange(half, dtype=jnp.int32)
    within, rest = place % share, place // share
    y, apart = rest % ny, rest // ny
    x_wide = (apart // bx) ^ lax.axis_index("wide_x")
    x_blk = (apart % bx) ^ lax.axis_index("blk_x")
    feature = (((y * nx + x_wide) * 2 + core) * bx + x_blk) * share + within
    return (jnp.arange(feature_count, dtype=jnp.int32)[:, None] == feature[None, :]).astype(BF16)


def shards(audio, video, owner, clip_feats, lengths, proj_weight):
    clips, features = audio.shape
    blocks = lax.axis_size(BLK)
    factor = 4.0 / blocks
    z, core = lax.axis_index("blk_z"), lax.axis_index("wide_c")
    nz = lax.axis_size("blk_z")

    audio_line = lax.all_gather(audio, "blk_z", axis=0, tiled=True)
    video_line = lax.all_gather(video, "blk_z", axis=0, tiled=True)

    peers = lax.axis_size(WIDE)
    slots = clip_feats.shape[0]
    capacity = slots // peers
    length_scale = lax.rsqrt(lengths.astype(F32))[:, None]
    pooled = (clip_feats.astype(F32) * length_scale).astype(BF16)
    pooled_slots = lax.all_to_all(
        pooled.reshape(peers, capacity, features), WIDE, 0, 0, tiled=True
    ).reshape(slots, features)
    both = swapped(jnp.concatenate([video, audio]), "blk_x")
    video_pair = jnp.concatenate([video, both[:clips]])
    audio_pair = jnp.concatenate([audio, both[clips:]])
    slope_own = gelu_slope(plain_dot(pooled, proj_weight))

    placing = placing_of(owner, slots, capacity)
    clip_rows = cols_dot(placing, pooled_slots).astype(BF16)
    row_pair = jnp.concatenate([clip_rows, swapped(clip_rows, "blk_x")])
    slope_pair = gelu_slope(plain_dot(row_pair, proj_weight))
    picked = plain_dot(row_pair, picking_of(core, features)).astype(BF16)
    other = plain_dot(row_pair, picking_of(1 - core, features)).astype(BF16)
    picked = jnp.concatenate([picked, swapped(other, "wide_c")])

    audio_line, slope_pair, picked, slope_own, placing = lax.optimization_barrier(
        (audio_line, slope_pair, picked, slope_own, placing)
    )

    row_ids = jnp.arange(nz * clips, dtype=jnp.int32)[:, None]
    col_ids = jnp.arange(2 * clips, dtype=jnp.int32)[None, :]
    labels = ((row_ids == z * clips + col_ids) & (col_ids < clips)).astype(F32)
    coeffs = pair_coeffs(rows_dot(audio_line, video_pair), labels, factor)
    video_part = cols_dot(coeffs, audio_line)

    pre_part = (video_part * slope_pair).astype(BF16)
    video_part, pre_part = lax.optimization_barrier((video_part, pre_part))
    pre_both = jnp.concatenate([pre_part, swapped(pre_part, "wide_c")])
    ny = lax.axis_size("wide_y")
    share = features // 8
    blocks_of = [
        cols_dot(picked[:, d * share : (d + 1) * share], pre_both) for d in range(4)
    ]
    summed = blocks_of[0]
    for d in (2, 1, 3):
        pairs = [(place, place ^ d) for place in range(4)]
        summed = summed + lax.ppermute(
            blocks_of[d].astype(BF16), ("wide_x", "blk_x"), pairs
        ).astype(F32)
    summed = summed.astype(BF16)

    arrived = swapped(video_part[clips:].astype(BF16), "blk_x")
    arrived, _ = lax.optimization_barrier((arrived, blocks_of))
    video_grad = (video_part[:clips] + arrived.astype(F32)).astype(BF16)
    packed = plain_dot(placing, video_grad).astype(BF16)
    received = lax.all_to_all(
        packed.reshape(peers, capacity, features), WIDE, 0, 0, tiled=True
    ).reshape(slots, features)
    summed, received = lax.optimization_barrier((summed, received))
    pre_grad = (received.astype(F32) * slope_own).astype(BF16)
    feats_grad = (rows_dot(pre_grad, proj_weight) * length_scale).astype(BF16)

    rows, cols = summed.shape[0] // ny, features // nz
    summed = summed.reshape(ny, rows, nz, cols).transpose(0, 2, 1, 3).reshape(ny * nz, rows, cols)
    pieces = lax.all_to_all(summed, ("wide_y", "blk_z"), 0, 0, tiled=True)
    video_line, summed = lax.optimization_barrier((video_line, summed))
    coeffs = pair_coeffs(rows_dot(audio_pair, video_line), labels.T, factor)
    audio_part = plain_dot(coeffs, video_line)
    audio_part, pieces = lax.optimization_barrier((audio_part, pieces))
    arrived = swapped(audio_part[clips:].astype(BF16), "blk_x")
    total = jnp.sum(pieces.astype(F32), axis=0).astype(BF16)
    gathered = lax.all_to_all(
        jnp.broadcast_to(total[None], (blocks, rows, cols)), BLK, 0, 0, tiled=True
    )

    arrived, gathered = lax.optimization_barrier((arrived, gathered))
    audio_grad = (audio_part[:clips] + arrived.astype(F32)).astype(BF16)
    weight_grad = (
        gathered.reshape(-1, nz, rows, cols).transpose(0, 2, 1, 3).reshape(-1, features).astype(F32)
    )
    return (audio_grad, feats_grad, weight_grad)


def solution(mesh):
    finer = Mesh(mesh.devices.reshape(8, 2, 2, 2, 8), AXES)
    rows = P(AXES, None)
    return jax.shard_map(
        shards,
        mesh=finer,
        in_specs=(rows, rows, rows, rows, P(AXES), P()),
        out_specs=(rows, rows, P(WIDE, None)),
        check_vma=False,
    )
```

```python
import jax
import jax.numpy as jnp
from jax import lax
from jax.experimental import pallas as pl
from jax.experimental.pallas import tpu as pltpu
from jax.sharding import Mesh
from jax.sharding import PartitionSpec as P

AXES = ("wide_y", "wide_x", "wide_c", "blk_x", "blk_z")
WIDE = ("wide_y", "wide_x", "wide_c")
BLK = ("blk_x", "blk_z")
BF16 = jnp.bfloat16
F32 = jnp.float32
ROOM = pltpu.CompilerParams(vmem_limit_bytes=40 * 2**20)
SCALAR = pl.BlockSpec(memory_space=pltpu.SMEM)


def swapped(array, axis):
    return lax.ppermute(array, axis, [(0, 1), (1, 0)])


def dot_of(matrix_a, matrix_b, dim_a, dim_b):
    return lax.dot_general(
        matrix_a, matrix_b, (((dim_a,), (dim_b,)), ((), ())), preferred_element_type=F32
    )


def gelu_slope(v):
    cdf = 0.5 * (1.0 + lax.erf(v * 0.7071067811865476))
    return cdf + v * (0.3989422804014327 * jnp.exp(-0.5 * v * v))


def targets_of(owner, capacity):
    ids = jnp.arange(owner.shape[0], dtype=jnp.int32)
    peer = owner[:, 0]
    before = (peer[:, None] == peer[None, :]) & (ids[:, None] < ids[None, :])
    return peer * capacity + jnp.sum(before.astype(jnp.int32), axis=0)


def picking_of(core, feature_count):
    half = feature_count // 2
    ny, nx = lax.axis_size("wide_y"), lax.axis_size("wide_x")
    bx = lax.axis_size("blk_x")
    share = half // (ny * nx * bx)
    place = jnp.arange(half, dtype=jnp.int32)
    within, rest = place % share, place // share
    y, apart = rest % ny, rest // ny
    x_wide = (apart // bx) ^ lax.axis_index("wide_x")
    x_blk = (apart % bx) ^ lax.axis_index("blk_x")
    feature = (((y * nx + x_wide) * 2 + core) * bx + x_blk) * share + within
    return (jnp.arange(feature_count, dtype=jnp.int32)[:, None] == feature[None, :]).astype(BF16)


def pair_kernel(factor, place_ref, line_ref, own_ref, mate_ref, kept_ref, sent_ref, line_grad_ref, total):
    step = pl.program_id(0)
    rows, clips = line_ref.shape[0], own_ref.shape[0]
    line = line_ref[...]
    video = jnp.concatenate([own_ref[...], mate_ref[...]], axis=0)
    scores = dot_of(video, line, 1, 1)
    row = lax.broadcasted_iota(jnp.int32, scores.shape, 0)
    col = lax.broadcasted_iota(jnp.int32, scores.shape, 1) + step * rows
    labels = ((col == place_ref[0] * clips + row) & (row < clips)).astype(F32)
    coeffs = (factor * (jax.nn.sigmoid(4.0 * scores - 2.0) - labels)).astype(BF16)
    part = dot_of(coeffs, line, 1, 0)

    @pl.when(step == 0)
    def _():
        total[...] = part

    @pl.when(step > 0)
    def _():
        total[...] += part

    line_grad_ref[...] = dot_of(coeffs, video, 0, 0).astype(BF16)

    @pl.when(step == pl.num_programs(0) - 1)
    def _():
        kept_ref[...] = total[:clips]
        sent_ref[...] = total[clips:].astype(BF16)


def pair_grads(line, own, mate, place, factor, steps):
    rows, features = line.shape
    clips = own.shape[0]
    whole = pl.BlockSpec((clips, features), lambda i: (0, 0))
    part = pl.BlockSpec((rows // steps, features), lambda i: (i, 0))
    return pl.pallas_call(
        lambda *refs: pair_kernel(factor, *refs),
        grid=(steps,),
        in_specs=[SCALAR, part, whole, whole],
        out_specs=[whole, whole, part],
        out_shape=[
            jax.ShapeDtypeStruct((clips, features), F32),
            jax.ShapeDtypeStruct((clips, features), BF16),
            jax.ShapeDtypeStruct((rows, features), BF16),
        ],
        scratch_shapes=[pltpu.VMEM((2 * clips, features), F32)],
        compiler_params=ROOM,
        cost_estimate=pl.CostEstimate(
            flops=12 * rows * clips * features, bytes_accessed=5 * rows * features, transcendentals=0
        ),
    )(place, line, own, mate)


def clip_kernel(kept_ref, arrived_ref, slope_ref, target_ref, packed_ref, pre_ref):
    grad = (kept_ref[...] + arrived_ref[...].astype(F32)).astype(BF16)
    pre_ref[...] = (grad.astype(F32) * slope_ref[...]).astype(BF16)
    slots, clips = packed_ref.shape[0], grad.shape[0]
    slot = lax.broadcasted_iota(jnp.int32, (slots, clips), 0)
    placing = (slot == target_ref[...]).astype(BF16)
    packed_ref[...] = dot_of(placing, grad, 1, 0).astype(BF16)


def clip_grads(kept, arrived, slope, targets, slots):
    clips, features = kept.shape
    return pl.pallas_call(
        clip_kernel,
        out_shape=[
            jax.ShapeDtypeStruct((slots, features), BF16),
            jax.ShapeDtypeStruct((clips, features), BF16),
        ],
        compiler_params=ROOM,
    )(kept, arrived, slope, targets[None, :])


def weight_kernel(own_picked, mate_picked, own_pre, mate_pre, *out_refs):
    share = out_refs[0].shape[0]
    picked = jnp.concatenate([own_picked[...], mate_picked[...]], axis=0)
    pre = jnp.concatenate([own_pre[...], mate_pre[...]], axis=0)
    product = dot_of(picked, pre, 0, 0)
    for d, out_ref in enumerate(out_refs):
        out_ref[...] = product[d * share : (d + 1) * share].astype(out_ref.dtype)


def weight_parts(own_picked, mate_picked, own_pre, mate_pre, count):
    half, features = own_picked.shape[1], own_pre.shape[1]
    shape = (half // count, features)
    return pl.pallas_call(
        weight_kernel,
        out_shape=[jax.ShapeDtypeStruct(shape, F32 if d == 0 else BF16) for d in range(count)],
        compiler_params=ROOM,
    )(own_picked, mate_picked, own_pre, mate_pre)


def shards(audio, video, owner, clip_feats, lengths, proj_weight):
    clips, features = audio.shape
    blocks = lax.axis_size(BLK)
    core = lax.axis_index("wide_c")
    place = lax.axis_index("blk_z").astype(jnp.int32)[None]
    audio_line = lax.all_gather(audio, "blk_z", axis=0, tiled=True)

    peers = lax.axis_size(WIDE)
    slots = clip_feats.shape[0]
    capacity = slots // peers
    length_scale = lax.rsqrt(lengths.astype(F32))[:, None]
    pooled = (clip_feats.astype(F32) * length_scale).astype(BF16)
    pooled_slots = lax.all_to_all(
        pooled.reshape(peers, capacity, features), WIDE, 0, 0, tiled=True
    ).reshape(slots, features)
    video_mate = swapped(video, "blk_x")
    slope_own = gelu_slope(dot_of(pooled, proj_weight, 1, 0))

    targets = targets_of(owner, capacity)
    placing = (targets[:, None] == jnp.arange(slots, dtype=jnp.int32)[None, :]).astype(BF16)
    clip_rows = dot_of(placing, pooled_slots, 1, 0).astype(BF16)
    slope_rows = gelu_slope(dot_of(clip_rows, proj_weight, 1, 0))
    picked = dot_of(clip_rows, picking_of(core, features), 1, 0).astype(BF16)
    picked_mate = swapped(
        dot_of(clip_rows, picking_of(1 - core, features), 1, 0).astype(BF16), "wide_c"
    )
    audio_line, video_mate, slope_rows, picked, picked_mate, slope_own, targets = (
        lax.optimization_barrier(
            (audio_line, video_mate, slope_rows, picked, picked_mate, slope_own, targets)
        )
    )

    kept, sent, line_grads = pair_grads(audio_line, video, video_mate, place, 4.0 / blocks, 4)
    audio_grad = lax.psum_scatter(line_grads, "blk_z", scatter_dimension=0, tiled=True)
    arrived = swapped(sent, "blk_x")
    packed, pre_rows = clip_grads(kept, arrived, slope_rows, targets, slots)
    received = lax.all_to_all(
        packed.reshape(peers, capacity, features), WIDE, 0, 0, tiled=True
    ).reshape(slots, features)

    pre_mate = swapped(pre_rows, "wide_c")
    parts = weight_parts(picked, picked_mate, pre_rows, pre_mate, 4)
    summed = parts[0]
    for d in (2, 1, 3):
        pairs = [(at, at ^ d) for at in range(4)]
        summed = summed + lax.ppermute(parts[d], ("wide_x", "blk_x"), pairs).astype(F32)
    summed = summed.astype(BF16)
    summed, received = lax.optimization_barrier((summed, received))
    ny = lax.axis_size("wide_y")
    pieces = lax.all_to_all(summed.reshape(ny, -1, features), "wide_y", 0, 0, tiled=True)
    pre_grad = (received.astype(F32) * slope_own).astype(BF16)
    feats_grad = (dot_of(pre_grad, proj_weight, 1, 1) * length_scale).astype(BF16)
    pieces, feats_grad = lax.optimization_barrier((pieces, feats_grad))
    total = jnp.sum(pieces.astype(F32), axis=0).astype(BF16)
    gathered = lax.all_to_all(
        jnp.broadcast_to(total[None], (blocks, *total.shape)), BLK, 0, 0, tiled=True
    )
    gathered = gathered.reshape(lax.axis_size("blk_x"), -1, *total.shape)
    weight_grad = jnp.sum(gathered.astype(F32), axis=1).reshape(-1, features)
    return (audio_grad, feats_grad, weight_grad)


def solution(mesh):
    finer = Mesh(mesh.devices.reshape(8, 2, 2, 2, 8), AXES)
    rows = P(AXES, None)
    return jax.shard_map(
        shards,
        mesh=finer,
        in_specs=(rows, rows, rows, rows, P(AXES), P()),
        out_specs=(rows, rows, P(WIDE, None)),
        check_vma=False,
    )
```

```python
import jax
import jax.numpy as jnp
from jax import lax
from jax.experimental import pallas as pl
from jax.experimental.pallas import tpu as pltpu
from jax.sharding import Mesh
from jax.sharding import PartitionSpec as P

AXES = ("wide_y", "wide_x", "wide_c", "blk_x", "blk_z")
WIDE = ("wide_y", "wide_x", "wide_c")
BLK = ("blk_x", "blk_z")
BF16 = jnp.bfloat16
F32 = jnp.float32
ROOM = pltpu.CompilerParams(vmem_limit_bytes=24 * 2**20)
ALL_ROOM = pltpu.CompilerParams(vmem_limit_bytes=56 * 2**20)
SCALAR = pl.BlockSpec(memory_space=pltpu.SMEM)


def swapped(array, axis):
    return lax.ppermute(array, axis, [(0, 1), (1, 0)])


def dot_of(matrix_a, matrix_b, dim_a, dim_b):
    return lax.dot_general(
        matrix_a, matrix_b, (((dim_a,), (dim_b,)), ((), ())), preferred_element_type=F32
    )


def gelu_slope(v):
    cdf = 0.5 * (1.0 + lax.erf(v * 0.7071067811865476))
    return cdf + v * (0.3989422804014327 * jnp.exp(-0.5 * v * v))


def targets_of(owner, capacity):
    ids = jnp.arange(owner.shape[0], dtype=jnp.int32)
    peer = owner[:, 0]
    before = (peer[:, None] == peer[None, :]) & (ids[:, None] < ids[None, :])
    return peer * capacity + jnp.sum(before.astype(jnp.int32), axis=0)


def picking_of(core, feature_count):
    half = feature_count // 2
    ny, nx = lax.axis_size("wide_y"), lax.axis_size("wide_x")
    bx = lax.axis_size("blk_x")
    share = half // (ny * nx * bx)
    place = jnp.arange(half, dtype=jnp.int32)
    within, rest = place % share, place // share
    y, apart = (rest + lax.axis_index("wide_y")) % ny, rest // ny
    x_wide = (apart // bx) ^ lax.axis_index("wide_x")
    x_blk = (apart % bx) ^ lax.axis_index("blk_x")
    feature = (((y * nx + x_wide) * 2 + core) * bx + x_blk) * share + within
    return (jnp.arange(feature_count, dtype=jnp.int32)[:, None] == feature[None, :]).astype(BF16)


def pair_kernel(factor, steps, place_ref, line_hbm, own_hbm, mate_hbm, slope_hbm,
                kept_ref, sent_ref, pre_ref, grads_hbm, line, video, slope, grads, total, came, gone):
    rows, clips = line.shape[0] // steps, own_hbm.shape[0]
    loads = [
        pltpu.make_async_copy(own_hbm, video.at[pl.ds(0, clips)], came.at[0]),
        pltpu.make_async_copy(mate_hbm, video.at[pl.ds(clips, clips)], came.at[1]),
    ]
    for step in range(steps):
        block = pl.ds(step * rows, rows)
        loads.append(pltpu.make_async_copy(line_hbm.at[block], line.at[block], came.at[2 + step]))
    loads.append(pltpu.make_async_copy(slope_hbm, slope, came.at[2 + steps]))
    for load in loads:
        load.start()
    loads[0].wait()
    loads[1].wait()
    stores = []
    for step in range(steps):
        block = pl.ds(step * rows, rows)
        loads[2 + step].wait()
        scores = dot_of(video[...], line[block], 1, 1)
        row = lax.broadcasted_iota(jnp.int32, scores.shape, 0)
        col = lax.broadcasted_iota(jnp.int32, scores.shape, 1) + step * rows
        labels = ((col == place_ref[0] * clips + row) & (row < clips)).astype(F32)
        coeffs = (factor * (jax.nn.sigmoid(4.0 * scores - 2.0) - labels)).astype(BF16)
        part = dot_of(coeffs, line[block], 1, 0)
        if step == 0:
            total[...] = part
        else:
            total[...] += part
        grads[block] = dot_of(coeffs, video[...], 0, 0).astype(BF16)
        stores.append(pltpu.make_async_copy(grads.at[block], grads_hbm.at[block], gone.at[step]))
        stores[-1].start()
    loads[-1].wait()
    kept_ref[...] = total[:clips]
    sent_ref[...] = total[clips:].astype(BF16)
    pre_ref[...] = (total[...] * slope[...]).astype(BF16)
    for store in stores:
        store.wait()


def pair_grads(line, own, mate, slope, place, factor, steps):
    rows, features = line.shape
    clips = own.shape[0]
    free = pl.BlockSpec(memory_space=pl.ANY)
    held = pl.BlockSpec(memory_space=pltpu.VMEM)
    return pl.pallas_call(
        lambda *refs: pair_kernel(factor, steps, *refs),
        in_specs=[SCALAR, free, free, free, free],
        out_specs=[held, held, held, free],
        out_shape=[
            jax.ShapeDtypeStruct((clips, features), F32),
            jax.ShapeDtypeStruct((clips, features), BF16),
            jax.ShapeDtypeStruct((2 * clips, features), BF16),
            jax.ShapeDtypeStruct((rows, features), BF16),
        ],
        scratch_shapes=[
            pltpu.VMEM((rows, features), BF16),
            pltpu.VMEM((2 * clips, features), BF16),
            pltpu.VMEM((2 * clips, features), F32),
            pltpu.VMEM((rows, features), BF16),
            pltpu.VMEM((2 * clips, features), F32),
            pltpu.SemaphoreType.DMA((3 + steps,)),
            pltpu.SemaphoreType.DMA((steps,)),
        ],
        compiler_params=ALL_ROOM,
        cost_estimate=pl.CostEstimate(
            flops=12 * rows * clips * features, bytes_accessed=5 * rows * features, transcendentals=0
        ),
    )(place, line, own, mate, slope)


def clip_kernel(kept_ref, arrived_ref, target_ref, packed_ref):
    grad = (kept_ref[...] + arrived_ref[...].astype(F32)).astype(BF16)
    slots, clips = packed_ref.shape[0], grad.shape[0]
    slot = lax.broadcasted_iota(jnp.int32, (slots, clips), 0)
    placing = (slot == target_ref[...]).astype(BF16)
    packed_ref[...] = dot_of(placing, grad, 1, 0).astype(BF16)


def clip_grads(kept, arrived, targets, slots):
    return pl.pallas_call(
        clip_kernel,
        out_shape=jax.ShapeDtypeStruct((slots, kept.shape[1]), BF16),
        compiler_params=ROOM,
        cost_estimate=pl.CostEstimate(flops=2 * 10**10, bytes_accessed=2**20, transcendentals=0),
    )(kept, arrived, targets[None, :])


def weight_kernel(own_picked, mate_picked, own_pre, mate_pre, *out_refs):
    share = out_refs[0].shape[0]
    for d, out_ref in enumerate(out_refs):
        block = pl.ds(d * share, share)
        product = dot_of(own_picked[block], own_pre[...], 1, 0)
        product += dot_of(mate_picked[block], mate_pre[...], 1, 0)
        out_ref[...] = product.astype(out_ref.dtype)


def weight_parts(own_picked, mate_picked, own_pre, mate_pre, count):
    half, features = own_picked.shape[0], own_pre.shape[1]
    shape = (half // count, features)
    return pl.pallas_call(
        weight_kernel,
        out_shape=[jax.ShapeDtypeStruct(shape, F32 if d == 0 else BF16) for d in range(count)],
        compiler_params=ROOM,
    )(own_picked, mate_picked, own_pre, mate_pre)


def sum_kernel(count, *refs):
    total = refs[0][...].astype(F32)
    for ref in refs[1:count]:
        total += ref[...].astype(F32)
    share = refs[count].shape[0]
    for s, out_ref in enumerate(refs[count:]):
        out_ref[...] = total[s * share : (s + 1) * share].astype(out_ref.dtype)


def sum_in_parts(arrays, parts):
    rows, features = arrays[0].shape
    return pl.pallas_call(
        lambda *refs: sum_kernel(len(arrays), *refs),
        out_shape=[
            jax.ShapeDtypeStruct((rows // parts, features), F32 if s == 0 else BF16)
            for s in range(parts)
        ],
        compiler_params=ROOM,
    )(*arrays)


def spread_kernel(count, *refs):
    total = refs[0][...].astype(F32)
    for ref in refs[1:count]:
        total += ref[...].astype(F32)
    refs[count][...] = jnp.broadcast_to(total.astype(BF16)[None], refs[count].shape)


def sum_spread(arrays, copies):
    return pl.pallas_call(
        lambda *refs: spread_kernel(len(arrays), *refs),
        out_shape=jax.ShapeDtypeStruct((copies, *arrays[0].shape), BF16),
        compiler_params=ROOM,
    )(*arrays)


def shards(audio, video, owner, clip_feats, lengths, proj_weight):
    clips, features = audio.shape
    blocks = lax.axis_size(BLK)
    core = lax.axis_index("wide_c")
    place = lax.axis_index("blk_z").astype(jnp.int32)[None]
    audio_line = lax.all_gather(audio, "blk_z", axis=0, tiled=True)

    peers = lax.axis_size(WIDE)
    slots = clip_feats.shape[0]
    capacity = slots // peers
    length_scale = lax.rsqrt(lengths.astype(F32))[:, None]
    pooled = (clip_feats.astype(F32) * length_scale).astype(BF16)
    pooled_slots = lax.all_to_all(
        pooled.reshape(peers, capacity, features), WIDE, 0, 0, tiled=True
    ).reshape(slots, features)
    video_mate = swapped(video, "blk_x")
    slope_own = gelu_slope(dot_of(pooled, proj_weight, 1, 0))

    targets = targets_of(owner, capacity)
    placing = (targets[:, None] == jnp.arange(slots, dtype=jnp.int32)[None, :]).astype(BF16)
    clip_rows = dot_of(placing, pooled_slots, 1, 0).astype(BF16)
    row_pair = jnp.concatenate([clip_rows, swapped(clip_rows, "blk_x")])
    slope_pair = gelu_slope(dot_of(row_pair, proj_weight, 1, 0))
    picked = dot_of(picking_of(core, features), row_pair, 0, 1).astype(BF16)
    picked_mate = swapped(
        dot_of(picking_of(1 - core, features), row_pair, 0, 1).astype(BF16), "wide_c"
    )
    audio_line, video_mate, slope_pair, picked, picked_mate, slope_own, targets = (
        lax.optimization_barrier(
            (audio_line, video_mate, slope_pair, picked, picked_mate, slope_own, targets)
        )
    )

    kept, sent, pre_pair, line_grads = pair_grads(
        audio_line, video, video_mate, slope_pair, place, 4.0 / blocks, 4
    )
    audio_grad = lax.psum_scatter(line_grads, "blk_z", scatter_dimension=0, tiled=True)

    pre_mate = swapped(pre_pair, "wide_c")
    arrived = swapped(sent, "blk_x")
    parts = weight_parts(picked, picked_mate, pre_pair, pre_mate, 4)
    came = [parts[0]]
    for d in (2, 1, 3):
        pairs = [(at, at ^ d) for at in range(4)]
        came.append(lax.ppermute(parts[d], ("wide_x", "blk_x"), pairs))

    arrived, parts = lax.optimization_barrier((arrived, parts))
    packed = clip_grads(kept, arrived, targets, slots)
    packed, came = lax.optimization_barrier((packed, came))
    received = lax.all_to_all(
        packed.reshape(peers, capacity, features), WIDE, 0, 0, tiled=True
    ).reshape(slots, features)

    packed, came = lax.optimization_barrier((packed, came))
    ny = lax.axis_size("wide_y")
    parts = sum_in_parts(came, ny)
    came = [parts[0]]
    for s in range(1, ny):
        pairs = [(at, (at + s) % ny) for at in range(ny)]
        came.append(lax.ppermute(parts[s], "wide_y", pairs))
    received, came = lax.optimization_barrier((received, came))
    total = sum_spread(came, blocks)
    gathered = lax.all_to_all(total, BLK, 0, 0, tiled=True)
    pre_grad = (received.astype(F32) * slope_own).astype(BF16)
    feats_grad = (dot_of(pre_grad, proj_weight, 1, 1) * length_scale).astype(BF16)
    gathered, feats_grad = lax.optimization_barrier((gathered, feats_grad))
    gathered = gathered.reshape(lax.axis_size("blk_x"), -1, *total.shape[1:])
    weight_grad = jnp.sum(gathered.astype(F32), axis=1).reshape(-1, features)
    return (audio_grad, feats_grad, weight_grad)


def solution(mesh):
    finer = Mesh(mesh.devices.reshape(8, 2, 2, 2, 8), AXES)
    rows = P(AXES, None)
    return jax.shard_map(
        shards,
        mesh=finer,
        in_specs=(rows, rows, rows, rows, P(AXES), P()),
        out_specs=(rows, rows, P(WIDE, None)),
        check_vma=False,
    )
```

```python
import jax
import jax.numpy as jnp
from jax import lax
from jax.experimental import pallas as pl
from jax.experimental.pallas import tpu as pltpu
from jax.sharding import Mesh
from jax.sharding import PartitionSpec as P

AXES = ("wide_y", "wide_x", "wide_c", "blk_x", "blk_z")
WIDE = ("wide_y", "wide_x", "wide_c")
BLK = ("blk_x", "blk_z")
BF16 = jnp.bfloat16
F32 = jnp.float32
ROOM = pltpu.CompilerParams(vmem_limit_bytes=24 * 2**20)
ALL_ROOM = pltpu.CompilerParams(vmem_limit_bytes=56 * 2**20)
SCALAR = pl.BlockSpec(memory_space=pltpu.SMEM)


def swapped(array, axis):
    return lax.ppermute(array, axis, [(0, 1), (1, 0)])


def dot_of(matrix_a, matrix_b, dim_a, dim_b):
    return lax.dot_general(
        matrix_a, matrix_b, (((dim_a,), (dim_b,)), ((), ())), preferred_element_type=F32
    )


def gelu_slope(v):
    cdf = 0.5 * (1.0 + lax.erf(v * 0.7071067811865476))
    return cdf + v * (0.3989422804014327 * jnp.exp(-0.5 * v * v))


def targets_of(owner, capacity):
    ids = jnp.arange(owner.shape[0], dtype=jnp.int32)
    peer = owner[:, 0]
    before = (peer[:, None] == peer[None, :]) & (ids[:, None] < ids[None, :])
    return peer * capacity + jnp.sum(before.astype(jnp.int32), axis=0)


def picking_of(core, feature_count):
    half = feature_count // 2
    ny, nx = lax.axis_size("wide_y"), lax.axis_size("wide_x")
    bx = lax.axis_size("blk_x")
    share = half // (ny * nx * bx)
    place = jnp.arange(half, dtype=jnp.int32)
    within, rest = place % share, place // share
    y, apart = rest % ny, rest // ny
    x_wide = (apart // bx) ^ lax.axis_index("wide_x")
    x_blk = (apart % bx) ^ lax.axis_index("blk_x")
    feature = (((y * nx + x_wide) * 2 + core) * bx + x_blk) * share + within
    return (jnp.arange(feature_count, dtype=jnp.int32)[:, None] == feature[None, :]).astype(BF16)


def pair_kernel(factor, steps, place_ref, line_hbm, own_hbm, mate_hbm, slope_hbm,
                kept_ref, sent_ref, pre_ref, grads_hbm, line, video, slope, grads, total, came, gone):
    rows, clips = line.shape[0] // steps, own_hbm.shape[0]
    loads = [
        pltpu.make_async_copy(own_hbm, video.at[pl.ds(0, clips)], came.at[0]),
        pltpu.make_async_copy(mate_hbm, video.at[pl.ds(clips, clips)], came.at[1]),
    ]
    for step in range(steps):
        block = pl.ds(step * rows, rows)
        loads.append(pltpu.make_async_copy(line_hbm.at[block], line.at[block], came.at[2 + step]))
    loads.append(pltpu.make_async_copy(slope_hbm, slope, came.at[2 + steps]))
    for load in loads:
        load.start()
    loads[0].wait()
    loads[1].wait()
    stores = []
    for step in range(steps):
        block = pl.ds(step * rows, rows)
        loads[2 + step].wait()
        scores = dot_of(video[...], line[block], 1, 1)
        row = lax.broadcasted_iota(jnp.int32, scores.shape, 0)
        col = lax.broadcasted_iota(jnp.int32, scores.shape, 1) + step * rows
        labels = ((col == place_ref[0] * clips + row) & (row < clips)).astype(F32)
        coeffs = (factor * (jax.nn.sigmoid(4.0 * scores - 2.0) - labels)).astype(BF16)
        part = dot_of(coeffs, line[block], 1, 0)
        if step == 0:
            total[...] = part
        else:
            total[...] += part
        grads[block] = dot_of(coeffs, video[...], 0, 0).astype(BF16)
        stores.append(pltpu.make_async_copy(grads.at[block], grads_hbm.at[block], gone.at[step]))
        stores[-1].start()
    loads[-1].wait()
    kept_ref[...] = total[:clips]
    sent_ref[...] = total[clips:].astype(BF16)
    pre_ref[...] = (total[...] * slope[...]).astype(BF16)
    for store in stores:
        store.wait()


def pair_grads(line, own, mate, slope, place, factor, steps):
    rows, features = line.shape
    clips = own.shape[0]
    free = pl.BlockSpec(memory_space=pl.ANY)
    held = pl.BlockSpec(memory_space=pltpu.VMEM)
    return pl.pallas_call(
        lambda *refs: pair_kernel(factor, steps, *refs),
        in_specs=[SCALAR, free, free, free, free],
        out_specs=[held, held, held, free],
        out_shape=[
            jax.ShapeDtypeStruct((clips, features), F32),
            jax.ShapeDtypeStruct((clips, features), BF16),
            jax.ShapeDtypeStruct((2 * clips, features), BF16),
            jax.ShapeDtypeStruct((rows, features), BF16),
        ],
        scratch_shapes=[
            pltpu.VMEM((rows, features), BF16),
            pltpu.VMEM((2 * clips, features), BF16),
            pltpu.VMEM((2 * clips, features), F32),
            pltpu.VMEM((rows, features), BF16),
            pltpu.VMEM((2 * clips, features), F32),
            pltpu.SemaphoreType.DMA((3 + steps,)),
            pltpu.SemaphoreType.DMA((steps,)),
        ],
        compiler_params=ALL_ROOM,
        cost_estimate=pl.CostEstimate(
            flops=12 * rows * clips * features, bytes_accessed=5 * rows * features, transcendentals=0
        ),
    )(place, line, own, mate, slope)


def clip_kernel(kept_ref, arrived_ref, target_ref, packed_ref):
    grad = (kept_ref[...] + arrived_ref[...].astype(F32)).astype(BF16)
    slots, clips = packed_ref.shape[0], grad.shape[0]
    slot = lax.broadcasted_iota(jnp.int32, (slots, clips), 0)
    placing = (slot == target_ref[...]).astype(BF16)
    packed_ref[...] = dot_of(placing, grad, 1, 0).astype(BF16)


def clip_grads(kept, arrived, targets, slots):
    return pl.pallas_call(
        clip_kernel,
        out_shape=jax.ShapeDtypeStruct((slots, kept.shape[1]), BF16),
        compiler_params=ROOM,
    )(kept, arrived, targets[None, :])


def weight_kernel(own_picked, mate_picked, own_pre, mate_pre, *out_refs):
    share = out_refs[0].shape[0]
    for d, out_ref in enumerate(out_refs):
        block = pl.ds(d * share, share)
        product = dot_of(own_picked[block], own_pre[...], 1, 0)
        product += dot_of(mate_picked[block], mate_pre[...], 1, 0)
        out_ref[...] = product.astype(out_ref.dtype)


def weight_parts(own_picked, mate_picked, own_pre, mate_pre, count):
    half, features = own_picked.shape[0], own_pre.shape[1]
    shape = (half // count, features)
    return pl.pallas_call(
        weight_kernel,
        out_shape=[jax.ShapeDtypeStruct(shape, F32 if d == 0 else BF16) for d in range(count)],
        compiler_params=ROOM,
    )(own_picked, mate_picked, own_pre, mate_pre)


def sum_kernel(*refs):
    total = refs[0][...].astype(F32)
    for ref in refs[1:-1]:
        total += ref[...].astype(F32)
    refs[-1][...] = total.astype(BF16)


def sum_of(arrays):
    return pl.pallas_call(
        sum_kernel,
        out_shape=jax.ShapeDtypeStruct(arrays[0].shape, BF16),
        compiler_params=ROOM,
    )(*arrays)


def spread_kernel(pieces_ref, out_ref):
    total = pieces_ref[0].astype(F32)
    for s in range(1, pieces_ref.shape[0]):
        total += pieces_ref[s].astype(F32)
    out_ref[...] = jnp.broadcast_to(total.astype(BF16)[None], out_ref.shape)


def sum_spread(pieces, copies):
    return pl.pallas_call(
        spread_kernel,
        out_shape=jax.ShapeDtypeStruct((copies, *pieces.shape[1:]), BF16),
        compiler_params=ROOM,
    )(pieces)


def shards(audio, video, owner, clip_feats, lengths, proj_weight):
    clips, features = audio.shape
    blocks = lax.axis_size(BLK)
    core = lax.axis_index("wide_c")
    place = lax.axis_index("blk_z").astype(jnp.int32)[None]
    audio_line = lax.all_gather(audio, "blk_z", axis=0, tiled=True)

    peers = lax.axis_size(WIDE)
    slots = clip_feats.shape[0]
    capacity = slots // peers
    length_scale = lax.rsqrt(lengths.astype(F32))[:, None]
    pooled = (clip_feats.astype(F32) * length_scale).astype(BF16)
    pooled_slots = lax.all_to_all(
        pooled.reshape(peers, capacity, features), WIDE, 0, 0, tiled=True
    ).reshape(slots, features)
    video_mate = swapped(video, "blk_x")
    slope_own = gelu_slope(dot_of(pooled, proj_weight, 1, 0))

    targets = targets_of(owner, capacity)
    placing = (targets[:, None] == jnp.arange(slots, dtype=jnp.int32)[None, :]).astype(BF16)
    clip_rows = dot_of(placing, pooled_slots, 1, 0).astype(BF16)
    row_pair = jnp.concatenate([clip_rows, swapped(clip_rows, "blk_x")])
    slope_pair = gelu_slope(dot_of(row_pair, proj_weight, 1, 0))
    picked = dot_of(picking_of(core, features), row_pair, 0, 1).astype(BF16)
    picked_mate = swapped(
        dot_of(picking_of(1 - core, features), row_pair, 0, 1).astype(BF16), "wide_c"
    )
    audio_line, video_mate, slope_pair, picked, picked_mate, slope_own, targets = (
        lax.optimization_barrier(
            (audio_line, video_mate, slope_pair, picked, picked_mate, slope_own, targets)
        )
    )

    kept, sent, pre_pair, line_grads = pair_grads(
        audio_line, video, video_mate, slope_pair, place, 4.0 / blocks, 4
    )
    audio_grad = lax.psum_scatter(line_grads, "blk_z", scatter_dimension=0, tiled=True)

    pre_mate = swapped(pre_pair, "wide_c")
    arrived = swapped(sent, "blk_x")
    parts = weight_parts(picked, picked_mate, pre_pair, pre_mate, 4)
    came = [parts[0]]
    for d in (2, 1, 3):
        pairs = [(at, at ^ d) for at in range(4)]
        came.append(lax.ppermute(parts[d], ("wide_x", "blk_x"), pairs))

    arrived, parts = lax.optimization_barrier((arrived, parts))
    packed = clip_grads(kept, arrived, targets, slots)
    received = lax.all_to_all(
        packed.reshape(peers, capacity, features), WIDE, 0, 0, tiled=True
    ).reshape(slots, features)

    packed, came = lax.optimization_barrier((packed, came))
    summed, received = lax.optimization_barrier((sum_of(came), received))
    pieces = lax.all_to_all(
        summed.reshape(lax.axis_size("wide_y"), -1, features), "wide_y", 0, 0, tiled=True
    )
    pre_grad = (received.astype(F32) * slope_own).astype(BF16)
    feats_grad = (dot_of(pre_grad, proj_weight, 1, 1) * length_scale).astype(BF16)
    pieces, feats_grad = lax.optimization_barrier((pieces, feats_grad))
    total = sum_spread(pieces, blocks)
    gathered = lax.all_to_all(total, BLK, 0, 0, tiled=True)
    gathered = gathered.reshape(lax.axis_size("blk_x"), -1, *total.shape[1:])
    weight_grad = jnp.sum(gathered.astype(F32), axis=1).reshape(-1, features)
    return (audio_grad, feats_grad, weight_grad)


def solution(mesh):
    finer = Mesh(mesh.devices.reshape(8, 2, 2, 2, 8), AXES)
    rows = P(AXES, None)
    return jax.shard_map(
        shards,
        mesh=finer,
        in_specs=(rows, rows, rows, rows, P(AXES), P()),
        out_specs=(rows, rows, P(WIDE, None)),
        check_vma=False,
    )
```

```python
import jax
import jax.numpy as jnp
from jax import lax
from jax.experimental import pallas as pl
from jax.experimental.pallas import tpu as pltpu
from jax.sharding import Mesh
from jax.sharding import PartitionSpec as P

AXES = ("wide_y", "wide_x", "wide_c", "blk_x", "blk_z")
WIDE = ("wide_y", "wide_x", "wide_c")
BLK = ("blk_x", "blk_z")
BF16 = jnp.bfloat16
F32 = jnp.float32
ROOM = pltpu.CompilerParams(vmem_limit_bytes=56 * 2**20)
SCALAR = pl.BlockSpec(memory_space=pltpu.SMEM)


def swapped(array, axis):
    return lax.ppermute(array, axis, [(0, 1), (1, 0)])


def dot_of(matrix_a, matrix_b, dim_a, dim_b):
    return lax.dot_general(
        matrix_a, matrix_b, (((dim_a,), (dim_b,)), ((), ())), preferred_element_type=F32
    )


def gelu_slope(v):
    cdf = 0.5 * (1.0 + lax.erf(v * 0.7071067811865476))
    return cdf + v * (0.3989422804014327 * jnp.exp(-0.5 * v * v))


def ranks_of(peer):
    ids = jnp.arange(peer.shape[0], dtype=jnp.int32)
    before = (peer[:, None] == peer[None, :]) & (ids[:, None] < ids[None, :])
    return jnp.sum(before.astype(jnp.int32), axis=0)


def order_of(slots, capacity):
    ny = lax.axis_size("wide_y")
    slot = jnp.arange(slots, dtype=jnp.int32)
    rank, source = slot % capacity, slot // capacity
    core = (source % 2) ^ lax.axis_index("wide_c")
    x = (source // 2 % 2) ^ lax.axis_index("wide_x")
    return ((source // 4 * 2 + core) * 2 + x) * capacity + rank


def picking_of(core, feature_count):
    half = feature_count // 2
    ny, nx = lax.axis_size("wide_y"), lax.axis_size("wide_x")
    bx = lax.axis_size("blk_x")
    share = half // (ny * nx * bx)
    place = jnp.arange(half, dtype=jnp.int32)
    within, rest = place % share, place // share
    y, x = rest % ny, rest // ny
    feature = (((y * nx + x // bx) * 2 + core) * bx + x % bx) * share + within
    return (jnp.arange(feature_count, dtype=jnp.int32)[:, None] == feature[None, :]).astype(BF16)


def pair_kernel(factor, steps, place_ref, line_hbm, own_hbm, mate_hbm, slope_hbm,
                kept_ref, sent_ref, pre_ref, coeffs_ref, line, video, slope, came):
    rows, clips = line.shape[0] // steps, own_hbm.shape[0]
    loads = [
        pltpu.make_async_copy(own_hbm, video.at[pl.ds(0, clips)], came.at[0]),
        pltpu.make_async_copy(mate_hbm, video.at[pl.ds(clips, clips)], came.at[1]),
    ]
    for step in range(steps):
        block = pl.ds(step * rows, rows)
        loads.append(pltpu.make_async_copy(line_hbm.at[block], line.at[block], came.at[2 + step]))
    loads.append(pltpu.make_async_copy(slope_hbm, slope, came.at[2 + steps]))
    for load in loads:
        load.start()
    loads[0].wait()
    loads[1].wait()
    for step in range(steps):
        block = pl.ds(step * rows, rows)
        loads[2 + step].wait()
        scores = dot_of(video[...], line[block], 1, 1)
        row = lax.broadcasted_iota(jnp.int32, scores.shape, 0)
        col = lax.broadcasted_iota(jnp.int32, scores.shape, 1) + step * rows
        labels = ((col == place_ref[0] * clips + row) & (row < clips)).astype(F32)
        coeffs = factor * (jax.nn.sigmoid(4.0 * scores - 2.0) - labels)
        coeffs_ref[:, block] = coeffs.astype(BF16)
    loads[-1].wait()
    total = dot_of(coeffs_ref[...], line[...], 1, 0)
    kept_ref[...] = total[:clips]
    sent_ref[...] = total[clips:].astype(BF16)
    pre_ref[...] = (total * slope[...]).astype(BF16)


def pair_grads(line, own, mate, slope, place, factor, steps):
    rows, features = line.shape
    clips = own.shape[0]
    free = pl.BlockSpec(memory_space=pl.ANY)
    return pl.pallas_call(
        lambda *refs: pair_kernel(factor, steps, *refs),
        in_specs=[SCALAR, free, free, free, free],
        out_shape=[
            jax.ShapeDtypeStruct((clips, features), F32),
            jax.ShapeDtypeStruct((clips, features), BF16),
            jax.ShapeDtypeStruct((2 * clips, features), BF16),
            jax.ShapeDtypeStruct((2 * clips, rows), BF16),
        ],
        scratch_shapes=[
            pltpu.VMEM((rows, features), BF16),
            pltpu.VMEM((2 * clips, features), BF16),
            pltpu.VMEM((2 * clips, features), F32),
            pltpu.SemaphoreType.DMA((3 + steps,)),
        ],
        compiler_params=ROOM,
        cost_estimate=pl.CostEstimate(
            flops=8 * rows * clips * features, bytes_accessed=3 * rows * features, transcendentals=0
        ),
    )(place, line, own, mate, slope)


def line_kernel(coeffs_ref, own_ref, mate_ref, out_ref):
    clips = own_ref.shape[0]
    total = dot_of(coeffs_ref[:clips], own_ref[...], 0, 0)
    total += dot_of(coeffs_ref[clips:], mate_ref[...], 0, 0)
    out_ref[...] = total.astype(BF16)


def line_grads_of(coeffs, own, mate, steps):
    pairs, rows = coeffs.shape
    clips, features = own.shape
    whole = pl.BlockSpec((clips, features), lambda i: (0, 0))
    return pl.pallas_call(
        line_kernel,
        grid=(steps,),
        in_specs=[pl.BlockSpec((pairs, rows // steps), lambda i: (0, i)), whole, whole],
        out_specs=pl.BlockSpec((rows // steps, features), lambda i: (i, 0)),
        out_shape=jax.ShapeDtypeStruct((rows, features), BF16),
        compiler_params=ROOM,
        cost_estimate=pl.CostEstimate(
            flops=4 * rows * clips * features, bytes_accessed=3 * rows * features, transcendentals=0
        ),
    )(coeffs, own, mate)


def clip_kernel(kept_ref, arrived_ref, place_ref, stay_ref, core_ref):
    grad = (kept_ref[...] + arrived_ref[...].astype(F32)).astype(BF16)
    slots, clips = stay_ref.shape[0], grad.shape[0]
    slot = lax.broadcasted_iota(jnp.int32, (slots, clips), 0)
    stay_ref[...] = dot_of((slot == place_ref[...]).astype(BF16), grad, 1, 0).astype(BF16)
    core_ref[...] = dot_of((slot + slots == place_ref[...]).astype(BF16), grad, 1, 0).astype(BF16)


def clip_grads(kept, arrived, places, slots):
    shape = jax.ShapeDtypeStruct((slots // 2, kept.shape[1]), BF16)
    return pl.pallas_call(
        clip_kernel,
        out_shape=[shape, shape],
        compiler_params=ROOM,
    )(kept, arrived, places[None, :])


def weight_kernel(own_picked, mate_picked, own_pre, mate_pre, out_ref):
    product = dot_of(own_picked[...], own_pre[...], 1, 0)
    product += dot_of(mate_picked[...], mate_pre[...], 1, 0)
    out_ref[...] = product.astype(BF16)


def weight_part(own_picked, mate_picked, own_pre, mate_pre):
    return pl.pallas_call(
        weight_kernel,
        out_shape=jax.ShapeDtypeStruct((own_picked.shape[0], own_pre.shape[1]), BF16),
        compiler_params=ROOM,
    )(own_picked, mate_picked, own_pre, mate_pre)


def load_kernel(stay_ref, core_ref, x_ref, pieces_ref, out_ref):
    count, lines, features = out_ref.shape
    part = x_ref.shape[0] // 2
    cells = part // count

    def by_y(ref, at):
        return ref[pl.ds(at, part)].astype(F32).reshape(count, cells, features)

    first = jnp.concatenate([by_y(stay_ref, 0), by_y(x_ref, 0)], axis=1)
    out_ref[:, pl.ds(0, 2 * cells)] = first.astype(BF16)
    second = jnp.concatenate([by_y(core_ref, 0), by_y(x_ref, part)], axis=1)
    out_ref[:, pl.ds(2 * cells, 2 * cells)] = second.astype(BF16)
    total = pieces_ref[0].astype(F32)
    for s in range(1, pieces_ref.shape[0]):
        total += pieces_ref[s].astype(F32)
    rows = lines - 4 * cells
    out_ref[:, pl.ds(4 * cells, rows)] = total.reshape(count, rows, features).astype(BF16)


def load_of(stay, core_in, x_in, pieces, count):
    lines = (2 * stay.shape[0] + pieces.shape[1]) // count
    return pl.pallas_call(
        load_kernel,
        out_shape=jax.ShapeDtypeStruct((count, lines, stay.shape[1]), BF16),
        compiler_params=ROOM,
    )(stay, core_in, x_in, pieces)


def spread_kernel(pieces_ref, out_ref):
    total = pieces_ref[0].astype(F32)
    for s in range(1, pieces_ref.shape[0]):
        total += pieces_ref[s].astype(F32)
    out_ref[...] = jnp.broadcast_to(total.astype(BF16)[None], out_ref.shape)


def sum_spread(pieces, rows, copies):
    count, lines, features = pieces.shape
    return pl.pallas_call(
        spread_kernel,
        grid=(1,),
        in_specs=[pl.BlockSpec((count, rows, features), lambda i: (0, lines // rows - 1, 0))],
        out_specs=pl.BlockSpec((copies, rows, features), lambda i: (0, 0, 0)),
        out_shape=jax.ShapeDtypeStruct((copies, rows, features), BF16),
        compiler_params=ROOM,
    )(pieces)


def shards(audio, video, owner, clip_feats, lengths, proj_weight):
    clips, features = audio.shape
    blocks = lax.axis_size(BLK)
    core = lax.axis_index("wide_c")
    place = lax.axis_index("blk_z").astype(jnp.int32)[None]
    audio_line = lax.all_gather(audio, "blk_z", axis=0, tiled=True)

    peers = lax.axis_size(WIDE)
    slots = clip_feats.shape[0]
    capacity = slots // peers
    length_scale = lax.rsqrt(lengths.astype(F32))[:, None]
    pooled = (clip_feats.astype(F32) * length_scale).astype(BF16)
    pooled_slots = lax.all_to_all(
        pooled.reshape(peers, capacity, features), WIDE, 0, 0, tiled=True
    ).reshape(slots, features)
    video_mate = swapped(video, "blk_x")
    slope_own = gelu_slope(dot_of(pooled, proj_weight, 1, 0))

    peer = owner[:, 0]
    ranks = ranks_of(peer)
    slot_of = peer * capacity + ranks
    placing = (slot_of[:, None] == jnp.arange(slots, dtype=jnp.int32)[None, :]).astype(BF16)
    ny = lax.axis_size("wide_y")
    core_apart = (peer % 2) ^ core
    x_apart = (peer // 2 % 2) ^ lax.axis_index("wide_x")
    places = ((core_apart * 2 + x_apart) * ny + peer // 4) * capacity + ranks
    clip_rows = dot_of(placing, pooled_slots, 1, 0).astype(BF16)
    row_pair = jnp.concatenate([clip_rows, swapped(clip_rows, "blk_x")])
    slope_pair = gelu_slope(dot_of(row_pair, proj_weight, 1, 0))
    picked = dot_of(picking_of(core, features), row_pair, 0, 1).astype(BF16)
    picked_mate = swapped(
        dot_of(picking_of(1 - core, features), row_pair, 0, 1).astype(BF16), "wide_c"
    )
    audio_line, video_mate, slope_pair, picked, picked_mate, slope_own, places = (
        lax.optimization_barrier(
            (audio_line, video_mate, slope_pair, picked, picked_mate, slope_own, places)
        )
    )

    kept, sent, pre_pair, coeffs = pair_grads(
        audio_line, video, video_mate, slope_pair, place, 4.0 / blocks, 4
    )

    pre_mate = swapped(pre_pair, "wide_c")
    arrived = swapped(sent, "blk_x")
    weight_sum = weight_part(picked, picked_mate, pre_pair, pre_mate)
    pieces = lax.all_to_all(
        weight_sum.reshape(4, -1, features), ("wide_x", "blk_x"), 0, 0, tiled=True
    )

    arrived, weight_sum = lax.optimization_barrier((arrived, weight_sum))
    stay, core_out = clip_grads(kept, arrived, places, slots)
    core_in = swapped(core_out, "wide_c")

    coeffs, core_in = lax.optimization_barrier((coeffs, core_in))
    line_grads = line_grads_of(coeffs, video, video_mate, 4)
    audio_grad = lax.psum_scatter(line_grads, "blk_z", scatter_dimension=0, tiled=True)

    part = slots // 4
    x_in = swapped(jnp.concatenate([stay[part:], core_in[part:]]), "wide_x")
    rows = pieces.shape[1] // ny
    load = load_of(stay, core_in, x_in, pieces, ny)
    load = lax.all_to_all(load, "wide_y", 0, 0, tiled=True)
    total = sum_spread(load, rows, blocks)
    gathered = lax.all_to_all(total, BLK, 0, 0, tiled=True)
    order = order_of(slots, capacity)
    sorting = (order[:, None] == jnp.arange(slots, dtype=jnp.int32)[None, :]).astype(BF16)
    received = dot_of(sorting, load[:, :-rows].reshape(slots, features), 1, 0)
    pre_grad = (received * slope_own).astype(BF16)
    feats_grad = (dot_of(pre_grad, proj_weight, 1, 1) * length_scale).astype(BF16)
    gathered, feats_grad = lax.optimization_barrier((gathered, feats_grad))
    gathered = gathered.reshape(lax.axis_size("blk_x"), -1, *total.shape[1:])
    weight_grad = jnp.sum(gathered.astype(F32), axis=1).reshape(-1, features)
    return (audio_grad, feats_grad, weight_grad)


def solution(mesh):
    finer = Mesh(mesh.devices.reshape(8, 2, 2, 2, 8), AXES)
    rows = P(AXES, None)
    return jax.shard_map(
        shards,
        mesh=finer,
        in_specs=(rows, rows, rows, rows, P(AXES), P()),
        out_specs=(rows, rows, P(WIDE, None)),
        check_vma=False,
    )
```

```python
import jax
import jax.numpy as jnp
from jax import lax
from jax.experimental import pallas as pl
from jax.experimental.pallas import tpu as pltpu
from jax.sharding import Mesh
from jax.sharding import PartitionSpec as P

AXES = ("wide_y", "wide_x", "wide_c", "blk_x", "blk_z")
WIDE = ("wide_y", "wide_x", "wide_c")
BLK = ("blk_x", "blk_z")
BF16 = jnp.bfloat16
F32 = jnp.float32
ROOM = pltpu.CompilerParams(vmem_limit_bytes=24 * 2**20)
ALL_ROOM = pltpu.CompilerParams(vmem_limit_bytes=56 * 2**20)
SCALAR = pl.BlockSpec(memory_space=pltpu.SMEM)


def swapped(array, axis):
    return lax.ppermute(array, axis, [(0, 1), (1, 0)])


def dot_of(matrix_a, matrix_b, dim_a, dim_b):
    return lax.dot_general(
        matrix_a, matrix_b, (((dim_a,), (dim_b,)), ((), ())), preferred_element_type=F32
    )


def gelu_slope(v):
    cdf = 0.5 * (1.0 + lax.erf(v * 0.7071067811865476))
    return cdf + v * (0.3989422804014327 * jnp.exp(-0.5 * v * v))


def targets_of(owner, capacity):
    ids = jnp.arange(owner.shape[0], dtype=jnp.int32)
    peer = owner[:, 0]
    before = (peer[:, None] == peer[None, :]) & (ids[:, None] < ids[None, :])
    return peer * capacity + jnp.sum(before.astype(jnp.int32), axis=0)


def picking_of(core, feature_count):
    half = feature_count // 2
    ny, nx = lax.axis_size("wide_y"), lax.axis_size("wide_x")
    bx = lax.axis_size("blk_x")
    share = half // (ny * nx * bx)
    place = jnp.arange(half, dtype=jnp.int32)
    within, rest = place % share, place // share
    y, x = rest % ny, rest // ny
    feature = (((y * nx + x // bx) * 2 + core) * bx + x % bx) * share + within
    return (jnp.arange(feature_count, dtype=jnp.int32)[:, None] == feature[None, :]).astype(BF16)


def pair_kernel(factor, steps, place_ref, line_hbm, own_hbm, mate_hbm, slope_hbm,
                kept_ref, sent_ref, pre_ref, grads_hbm, line, video, slope, grads, total, came, gone):
    rows, clips = line.shape[0] // steps, own_hbm.shape[0]
    loads = [
        pltpu.make_async_copy(own_hbm, video.at[pl.ds(0, clips)], came.at[0]),
        pltpu.make_async_copy(mate_hbm, video.at[pl.ds(clips, clips)], came.at[1]),
    ]
    for step in range(steps):
        block = pl.ds(step * rows, rows)
        loads.append(pltpu.make_async_copy(line_hbm.at[block], line.at[block], came.at[2 + step]))
    loads.append(pltpu.make_async_copy(slope_hbm, slope, came.at[2 + steps]))
    for load in loads:
        load.start()
    loads[0].wait()
    loads[1].wait()

    def coeffs_of(step):
        block = pl.ds(step * rows, rows)
        loads[2 + step].wait()
        scores = dot_of(video[...], line[block], 1, 1)
        row = lax.broadcasted_iota(jnp.int32, scores.shape, 0)
        col = lax.broadcasted_iota(jnp.int32, scores.shape, 1) + step * rows
        labels = ((col == place_ref[0] * clips + row) & (row < clips)).astype(F32)
        return (factor * (jax.nn.sigmoid(4.0 * scores - 2.0) - labels)).astype(BF16)

    stores = []
    coeffs = coeffs_of(0)
    for step in range(steps):
        block = pl.ds(step * rows, rows)
        ready = coeffs
        if step + 1 < steps:
            coeffs = coeffs_of(step + 1)
        part = dot_of(ready, line[block], 1, 0)
        if step == 0:
            total[...] = part
        else:
            total[...] += part
        grads[block] = dot_of(ready, video[...], 0, 0).astype(BF16)
        stores.append(pltpu.make_async_copy(grads.at[block], grads_hbm.at[block], gone.at[step]))
        stores[-1].start()
    loads[-1].wait()
    kept_ref[...] = total[:clips]
    sent_ref[...] = total[clips:].astype(BF16)
    pre_ref[...] = (total[...] * slope[...]).astype(BF16)
    for store in stores:
        store.wait()


def pair_grads(line, own, mate, slope, place, factor, steps):
    rows, features = line.shape
    clips = own.shape[0]
    free = pl.BlockSpec(memory_space=pl.ANY)
    held = pl.BlockSpec(memory_space=pltpu.VMEM)
    return pl.pallas_call(
        lambda *refs: pair_kernel(factor, steps, *refs),
        in_specs=[SCALAR, free, free, free, free],
        out_specs=[held, held, held, free],
        out_shape=[
            jax.ShapeDtypeStruct((clips, features), F32),
            jax.ShapeDtypeStruct((clips, features), BF16),
            jax.ShapeDtypeStruct((2 * clips, features), BF16),
            jax.ShapeDtypeStruct((rows, features), BF16),
        ],
        scratch_shapes=[
            pltpu.VMEM((rows, features), BF16),
            pltpu.VMEM((2 * clips, features), BF16),
            pltpu.VMEM((2 * clips, features), F32),
            pltpu.VMEM((rows, features), BF16),
            pltpu.VMEM((2 * clips, features), F32),
            pltpu.SemaphoreType.DMA((3 + steps,)),
            pltpu.SemaphoreType.DMA((steps,)),
        ],
        compiler_params=ALL_ROOM,
        cost_estimate=pl.CostEstimate(
            flops=12 * rows * clips * features, bytes_accessed=5 * rows * features, transcendentals=0
        ),
    )(place, line, own, mate, slope)


def clip_kernel(kept_ref, arrived_ref, target_ref, packed_ref):
    grad = (kept_ref[...] + arrived_ref[...].astype(F32)).astype(BF16)
    slots, clips = packed_ref.shape[0], grad.shape[0]
    slot = lax.broadcasted_iota(jnp.int32, (slots, clips), 0)
    placing = (slot == target_ref[...]).astype(BF16)
    packed_ref[...] = dot_of(placing, grad, 1, 0).astype(BF16)


def clip_grads(kept, arrived, targets, slots):
    return pl.pallas_call(
        clip_kernel,
        out_shape=jax.ShapeDtypeStruct((slots, kept.shape[1]), BF16),
        compiler_params=ROOM,
    )(kept, arrived, targets[None, :])


def weight_kernel(own_picked, mate_picked, own_pre, mate_pre, out_ref):
    product = dot_of(own_picked[...], own_pre[...], 1, 0)
    product += dot_of(mate_picked[...], mate_pre[...], 1, 0)
    out_ref[...] = product.astype(BF16)


def weight_part(own_picked, mate_picked, own_pre, mate_pre):
    return pl.pallas_call(
        weight_kernel,
        out_shape=jax.ShapeDtypeStruct((own_picked.shape[0], own_pre.shape[1]), BF16),
        compiler_params=ROOM,
    )(own_picked, mate_picked, own_pre, mate_pre)


def sum_kernel(pieces_ref, out_ref):
    total = pieces_ref[0].astype(F32)
    for s in range(1, pieces_ref.shape[0]):
        total += pieces_ref[s].astype(F32)
    out_ref[...] = total.astype(BF16)


def sum_of(pieces):
    return pl.pallas_call(
        sum_kernel,
        out_shape=jax.ShapeDtypeStruct(pieces.shape[1:], BF16),
        compiler_params=ROOM,
    )(pieces)


def spread_kernel(pieces_ref, out_ref):
    total = pieces_ref[0].astype(F32)
    for s in range(1, pieces_ref.shape[0]):
        total += pieces_ref[s].astype(F32)
    out_ref[...] = jnp.broadcast_to(total.astype(BF16)[None], out_ref.shape)


def sum_spread(pieces, copies):
    return pl.pallas_call(
        spread_kernel,
        out_shape=jax.ShapeDtypeStruct((copies, *pieces.shape[1:]), BF16),
        compiler_params=ROOM,
    )(pieces)


def shards(audio, video, owner, clip_feats, lengths, proj_weight):
    clips, features = audio.shape
    blocks = lax.axis_size(BLK)
    core = lax.axis_index("wide_c")
    place = lax.axis_index("blk_z").astype(jnp.int32)[None]
    audio_line = lax.all_gather(audio, "blk_z", axis=0, tiled=True)

    peers = lax.axis_size(WIDE)
    slots = clip_feats.shape[0]
    capacity = slots // peers
    length_scale = lax.rsqrt(lengths.astype(F32))[:, None]
    pooled = (clip_feats.astype(F32) * length_scale).astype(BF16)
    pooled_slots = lax.all_to_all(
        pooled.reshape(peers, capacity, features), WIDE, 0, 0, tiled=True
    ).reshape(slots, features)
    video_mate = swapped(video, "blk_x")
    slope_own = gelu_slope(dot_of(pooled, proj_weight, 1, 0))

    targets = targets_of(owner, capacity)
    placing = (targets[:, None] == jnp.arange(slots, dtype=jnp.int32)[None, :]).astype(BF16)
    clip_rows = dot_of(placing, pooled_slots, 1, 0).astype(BF16)
    row_pair = jnp.concatenate([clip_rows, swapped(clip_rows, "blk_x")])
    slope_pair = gelu_slope(dot_of(row_pair, proj_weight, 1, 0))
    picked = dot_of(picking_of(core, features), row_pair, 0, 1).astype(BF16)
    picked_mate = swapped(
        dot_of(picking_of(1 - core, features), row_pair, 0, 1).astype(BF16), "wide_c"
    )
    audio_line, video_mate, slope_pair, picked, picked_mate, slope_own, targets = (
        lax.optimization_barrier(
            (audio_line, video_mate, slope_pair, picked, picked_mate, slope_own, targets)
        )
    )

    kept, sent, pre_pair, line_grads = pair_grads(
        audio_line, video, video_mate, slope_pair, place, 4.0 / blocks, 4
    )
    audio_grad = lax.psum_scatter(line_grads, "blk_z", scatter_dimension=0, tiled=True)

    pre_mate = swapped(pre_pair, "wide_c")
    arrived = swapped(sent, "blk_x")
    weight_sum = weight_part(picked, picked_mate, pre_pair, pre_mate)
    pieces = lax.all_to_all(
        weight_sum.reshape(4, -1, features), ("wide_x", "blk_x"), 0, 0, tiled=True
    )

    arrived, pieces = lax.optimization_barrier((arrived, pieces))
    packed = clip_grads(kept, arrived, targets, slots)
    received = lax.all_to_all(
        packed.reshape(peers, capacity, features), WIDE, 0, 0, tiled=True
    ).reshape(slots, features)

    pieces, packed = lax.optimization_barrier((pieces, packed))
    summed, received = lax.optimization_barrier((sum_of(pieces), received))
    pieces = lax.all_to_all(
        summed.reshape(lax.axis_size("wide_y"), -1, features), "wide_y", 0, 0, tiled=True
    )
    pre_grad = (received.astype(F32) * slope_own).astype(BF16)
    feats_grad = (dot_of(pre_grad, proj_weight, 1, 1) * length_scale).astype(BF16)
    pieces, feats_grad = lax.optimization_barrier((pieces, feats_grad))
    total = sum_spread(pieces, blocks)
    gathered = lax.all_to_all(total, BLK, 0, 0, tiled=True)
    gathered = gathered.reshape(lax.axis_size("blk_x"), -1, *total.shape[1:])
    weight_grad = jnp.sum(gathered.astype(F32), axis=1).reshape(-1, features)
    return (audio_grad, feats_grad, weight_grad)


def solution(mesh):
    finer = Mesh(mesh.devices.reshape(8, 2, 2, 2, 8), AXES)
    rows = P(AXES, None)
    return jax.shard_map(
        shards,
        mesh=finer,
        in_specs=(rows, rows, rows, rows, P(AXES), P()),
        out_specs=(rows, rows, P(WIDE, None)),
        check_vma=False,
    )
```

```python
import jax
import jax.numpy as jnp
from jax import lax
from jax.experimental import pallas as pl
from jax.experimental.pallas import tpu as pltpu
from jax.sharding import Mesh
from jax.sharding import PartitionSpec as P

AXES = ("wide_y", "wide_x", "wide_c", "blk_x", "blk_z")
WIDE = ("wide_y", "wide_x", "wide_c")
BLK = ("blk_x", "blk_z")
BF16 = jnp.bfloat16
F32 = jnp.float32
ROOM = pltpu.CompilerParams(vmem_limit_bytes=24 * 2**20)
ALL_ROOM = pltpu.CompilerParams(vmem_limit_bytes=56 * 2**20)
SCALAR = pl.BlockSpec(memory_space=pltpu.SMEM)


def swapped(array, axis):
    return lax.ppermute(array, axis, [(0, 1), (1, 0)])


def dot_of(matrix_a, matrix_b, dim_a, dim_b):
    return lax.dot_general(
        matrix_a, matrix_b, (((dim_a,), (dim_b,)), ((), ())), preferred_element_type=F32
    )


def gelu_slope(v):
    cdf = 0.5 * (1.0 + lax.erf(v * 0.7071067811865476))
    return cdf + v * (0.3989422804014327 * jnp.exp(-0.5 * v * v))


def targets_of(owner, capacity):
    ids = jnp.arange(owner.shape[0], dtype=jnp.int32)
    peer = owner[:, 0]
    before = (peer[:, None] == peer[None, :]) & (ids[:, None] < ids[None, :])
    return peer * capacity + jnp.sum(before.astype(jnp.int32), axis=0)


def picking_of(core, feature_count):
    half = feature_count // 2
    ny, nx = lax.axis_size("wide_y"), lax.axis_size("wide_x")
    bx = lax.axis_size("blk_x")
    share = half // (ny * nx * bx)
    place = jnp.arange(half, dtype=jnp.int32)
    within, rest = place % share, place // share
    y, apart = rest % ny, rest // ny
    x_wide = (apart // bx) ^ lax.axis_index("wide_x")
    x_blk = (apart % bx) ^ lax.axis_index("blk_x")
    feature = (((y * nx + x_wide) * 2 + core) * bx + x_blk) * share + within
    return (jnp.arange(feature_count, dtype=jnp.int32)[:, None] == feature[None, :]).astype(BF16)


def pair_kernel(factor, steps, place_ref, line_hbm, own_hbm, mate_hbm,
                kept_ref, sent_ref, grads_hbm, line, video, grads, total, came, gone):
    rows, clips = line.shape[0] // steps, own_hbm.shape[0]
    loads = [
        pltpu.make_async_copy(own_hbm, video.at[pl.ds(0, clips)], came.at[0]),
        pltpu.make_async_copy(mate_hbm, video.at[pl.ds(clips, clips)], came.at[1]),
    ]
    for step in range(steps):
        block = pl.ds(step * rows, rows)
        loads.append(pltpu.make_async_copy(line_hbm.at[block], line.at[block], came.at[2 + step]))
    for load in loads:
        load.start()
    loads[0].wait()
    loads[1].wait()

    def coeffs_of(step):
        block = pl.ds(step * rows, rows)
        loads[2 + step].wait()
        scores = dot_of(video[...], line[block], 1, 1)
        row = lax.broadcasted_iota(jnp.int32, scores.shape, 0)
        col = lax.broadcasted_iota(jnp.int32, scores.shape, 1) + step * rows
        labels = ((col == place_ref[0] * clips + row) & (row < clips)).astype(F32)
        return (factor * (jax.nn.sigmoid(4.0 * scores - 2.0) - labels)).astype(BF16)

    stores = []
    coeffs = coeffs_of(0)
    for step in range(steps):
        block = pl.ds(step * rows, rows)
        ready = coeffs
        if step + 1 < steps:
            coeffs = coeffs_of(step + 1)
        part = dot_of(ready, line[block], 1, 0)
        if step == 0:
            total[...] = part
        else:
            total[...] += part
        grads[block] = dot_of(ready, video[...], 0, 0).astype(BF16)
        stores.append(pltpu.make_async_copy(grads.at[block], grads_hbm.at[block], gone.at[step]))
        stores[-1].start()
    kept_ref[...] = total[:clips]
    sent_ref[...] = total[clips:].astype(BF16)
    for store in stores:
        store.wait()


def pair_grads(line, own, mate, place, factor, steps):
    rows, features = line.shape
    clips = own.shape[0]
    free = pl.BlockSpec(memory_space=pl.ANY)
    held = pl.BlockSpec(memory_space=pltpu.VMEM)
    return pl.pallas_call(
        lambda *refs: pair_kernel(factor, steps, *refs),
        in_specs=[SCALAR, free, free, free],
        out_specs=[held, held, free],
        out_shape=[
            jax.ShapeDtypeStruct((clips, features), F32),
            jax.ShapeDtypeStruct((clips, features), BF16),
            jax.ShapeDtypeStruct((rows, features), BF16),
        ],
        scratch_shapes=[
            pltpu.VMEM((rows, features), BF16),
            pltpu.VMEM((2 * clips, features), BF16),
            pltpu.VMEM((rows, features), BF16),
            pltpu.VMEM((2 * clips, features), F32),
            pltpu.SemaphoreType.DMA((2 + steps,)),
            pltpu.SemaphoreType.DMA((steps,)),
        ],
        compiler_params=ALL_ROOM,
        cost_estimate=pl.CostEstimate(
            flops=12 * rows * clips * features, bytes_accessed=5 * rows * features, transcendentals=0
        ),
    )(place, line, own, mate)


def clip_kernel(kept_ref, arrived_ref, slope_ref, target_ref, packed_ref, pre_ref):
    grad = (kept_ref[...] + arrived_ref[...].astype(F32)).astype(BF16)
    pre_ref[...] = (grad.astype(F32) * slope_ref[...]).astype(BF16)
    slots, clips = packed_ref.shape[0], grad.shape[0]
    slot = lax.broadcasted_iota(jnp.int32, (slots, clips), 0)
    placing = (slot == target_ref[...]).astype(BF16)
    packed_ref[...] = dot_of(placing, grad, 1, 0).astype(BF16)


def clip_grads(kept, arrived, slope, targets, slots):
    clips, features = kept.shape
    return pl.pallas_call(
        clip_kernel,
        out_shape=[
            jax.ShapeDtypeStruct((slots, features), BF16),
            jax.ShapeDtypeStruct((clips, features), BF16),
        ],
        compiler_params=ROOM,
    )(kept, arrived, slope, targets[None, :])


def weight_kernel(own_picked, mate_picked, own_pre, mate_pre, *out_refs):
    share = out_refs[0].shape[0]
    picked = jnp.concatenate([own_picked[...], mate_picked[...]], axis=0)
    pre = jnp.concatenate([own_pre[...], mate_pre[...]], axis=0)
    product = dot_of(picked, pre, 0, 0)
    for d, out_ref in enumerate(out_refs):
        out_ref[...] = product[d * share : (d + 1) * share].astype(out_ref.dtype)


def weight_parts(own_picked, mate_picked, own_pre, mate_pre, count):
    half, features = own_picked.shape[1], own_pre.shape[1]
    shape = (half // count, features)
    return pl.pallas_call(
        weight_kernel,
        out_shape=[jax.ShapeDtypeStruct(shape, F32 if d == 0 else BF16) for d in range(count)],
        compiler_params=ROOM,
    )(own_picked, mate_picked, own_pre, mate_pre)


def shards(audio, video, owner, clip_feats, lengths, proj_weight):
    clips, features = audio.shape
    blocks = lax.axis_size(BLK)
    core = lax.axis_index("wide_c")
    place = lax.axis_index("blk_z").astype(jnp.int32)[None]
    audio_line = lax.all_gather(audio, "blk_z", axis=0, tiled=True)

    peers = lax.axis_size(WIDE)
    slots = clip_feats.shape[0]
    capacity = slots // peers
    length_scale = lax.rsqrt(lengths.astype(F32))[:, None]
    pooled = (clip_feats.astype(F32) * length_scale).astype(BF16)
    pooled_slots = lax.all_to_all(
        pooled.reshape(peers, capacity, features), WIDE, 0, 0, tiled=True
    ).reshape(slots, features)
    video_mate = swapped(video, "blk_x")
    slope_own = gelu_slope(dot_of(pooled, proj_weight, 1, 0))

    targets = targets_of(owner, capacity)
    placing = (targets[:, None] == jnp.arange(slots, dtype=jnp.int32)[None, :]).astype(BF16)
    clip_rows = dot_of(placing, pooled_slots, 1, 0).astype(BF16)
    slope_rows = gelu_slope(dot_of(clip_rows, proj_weight, 1, 0))
    picked = dot_of(clip_rows, picking_of(core, features), 1, 0).astype(BF16)
    picked_mate = swapped(
        dot_of(clip_rows, picking_of(1 - core, features), 1, 0).astype(BF16), "wide_c"
    )
    audio_line, video_mate, slope_rows, picked, picked_mate, slope_own, targets = (
        lax.optimization_barrier(
            (audio_line, video_mate, slope_rows, picked, picked_mate, slope_own, targets)
        )
    )

    kept, sent, line_grads = pair_grads(audio_line, video, video_mate, place, 4.0 / blocks, 4)
    audio_grad = lax.psum_scatter(line_grads, "blk_z", scatter_dimension=0, tiled=True)
    arrived = swapped(sent, "blk_x")
    packed, pre_rows = clip_grads(kept, arrived, slope_rows, targets, slots)
    received = lax.all_to_all(
        packed.reshape(peers, capacity, features), WIDE, 0, 0, tiled=True
    ).reshape(slots, features)

    pre_mate = swapped(pre_rows, "wide_c")
    parts = weight_parts(picked, picked_mate, pre_rows, pre_mate, 4)
    summed = parts[0]
    for d in (2, 1, 3):
        pairs = [(at, at ^ d) for at in range(4)]
        summed = summed + lax.ppermute(parts[d], ("wide_x", "blk_x"), pairs).astype(F32)
    summed = summed.astype(BF16)
    summed, received = lax.optimization_barrier((summed, received))
    ny = lax.axis_size("wide_y")
    pieces = lax.all_to_all(summed.reshape(ny, -1, features), "wide_y", 0, 0, tiled=True)
    pre_grad = (received.astype(F32) * slope_own).astype(BF16)
    feats_grad = (dot_of(pre_grad, proj_weight, 1, 1) * length_scale).astype(BF16)
    pieces, feats_grad = lax.optimization_barrier((pieces, feats_grad))
    total = jnp.sum(pieces.astype(F32), axis=0).astype(BF16)
    gathered = lax.all_to_all(
        jnp.broadcast_to(total[None], (blocks, *total.shape)), BLK, 0, 0, tiled=True
    )
    gathered = gathered.reshape(lax.axis_size("blk_x"), -1, *total.shape)
    weight_grad = jnp.sum(gathered.astype(F32), axis=1).reshape(-1, features)
    return (audio_grad, feats_grad, weight_grad)


def solution(mesh):
    finer = Mesh(mesh.devices.reshape(8, 2, 2, 2, 8), AXES)
    rows = P(AXES, None)
    return jax.shard_map(
        shards,
        mesh=finer,
        in_specs=(rows, rows, rows, rows, P(AXES), P()),
        out_specs=(rows, rows, P(WIDE, None)),
        check_vma=False,
    )
```

```python
import jax
import jax.numpy as jnp
from jax import lax
from jax.experimental import pallas as pl
from jax.experimental.pallas import tpu as pltpu
from jax.sharding import Mesh
from jax.sharding import PartitionSpec as P

AXES = ("wide_y", "wide_x", "wide_c", "blk_x", "blk_z")
WIDE = ("wide_y", "wide_x", "wide_c")
BLK = ("blk_x", "blk_z")
BF16 = jnp.bfloat16
F32 = jnp.float32
ROOM = pltpu.CompilerParams(vmem_limit_bytes=24 * 2**20)
ALL_ROOM = pltpu.CompilerParams(vmem_limit_bytes=56 * 2**20)
SCALAR = pl.BlockSpec(memory_space=pltpu.SMEM)


def swapped(array, axis):
    return lax.ppermute(array, axis, [(0, 1), (1, 0)])


def dot_of(matrix_a, matrix_b, dim_a, dim_b):
    return lax.dot_general(
        matrix_a, matrix_b, (((dim_a,), (dim_b,)), ((), ())), preferred_element_type=F32
    )


def gelu_slope(v):
    cdf = 0.5 * (1.0 + lax.erf(v * 0.7071067811865476))
    return cdf + v * (0.3989422804014327 * jnp.exp(-0.5 * v * v))


def ranks_of(peer):
    ids = jnp.arange(peer.shape[0], dtype=jnp.int32)
    before = (peer[:, None] == peer[None, :]) & (ids[:, None] < ids[None, :])
    return jnp.sum(before.astype(jnp.int32), axis=0)


def picking_of(core, feature_count):
    half = feature_count // 2
    ny, nx = lax.axis_size("wide_y"), lax.axis_size("wide_x")
    bx = lax.axis_size("blk_x")
    share = half // (ny * nx * bx)
    place = jnp.arange(half, dtype=jnp.int32)
    within, rest = place % share, place // share
    y, apart = rest % ny, rest // ny
    x_wide = (apart // bx) ^ lax.axis_index("wide_x")
    x_blk = (apart % bx) ^ lax.axis_index("blk_x")
    feature = (((y * nx + x_wide) * 2 + core) * bx + x_blk) * share + within
    return (jnp.arange(feature_count, dtype=jnp.int32)[:, None] == feature[None, :]).astype(BF16)


def pair_kernel(factor, steps, place_ref, line_hbm, own_hbm, mate_hbm,
                kept_ref, sent_ref, grads_hbm, line, video, grads, total, came, gone):
    rows, clips = line.shape[0] // steps, own_hbm.shape[0]
    loads = [
        pltpu.make_async_copy(own_hbm, video.at[pl.ds(0, clips)], came.at[0]),
        pltpu.make_async_copy(mate_hbm, video.at[pl.ds(clips, clips)], came.at[1]),
    ]
    for step in range(steps):
        block = pl.ds(step * rows, rows)
        loads.append(pltpu.make_async_copy(line_hbm.at[block], line.at[block], came.at[2 + step]))
    for load in loads:
        load.start()
    loads[0].wait()
    loads[1].wait()

    def coeffs_of(step):
        block = pl.ds(step * rows, rows)
        loads[2 + step].wait()
        scores = dot_of(video[...], line[block], 1, 1)
        row = lax.broadcasted_iota(jnp.int32, scores.shape, 0)
        col = lax.broadcasted_iota(jnp.int32, scores.shape, 1) + step * rows
        labels = ((col == place_ref[0] * clips + row) & (row < clips)).astype(F32)
        return (factor * (jax.nn.sigmoid(4.0 * scores - 2.0) - labels)).astype(BF16)

    stores = []
    coeffs = coeffs_of(0)
    for step in range(steps):
        block = pl.ds(step * rows, rows)
        ready = coeffs
        if step + 1 < steps:
            coeffs = coeffs_of(step + 1)
        part = dot_of(ready, line[block], 1, 0)
        if step == 0:
            total[...] = part
        else:
            total[...] += part
        grads[block] = dot_of(ready, video[...], 0, 0).astype(BF16)
        stores.append(pltpu.make_async_copy(grads.at[block], grads_hbm.at[block], gone.at[step]))
        stores[-1].start()
    kept_ref[...] = total[:clips]
    sent_ref[...] = total[clips:].astype(BF16)
    for store in stores:
        store.wait()


def pair_grads(line, own, mate, place, factor, steps):
    rows, features = line.shape
    clips = own.shape[0]
    free = pl.BlockSpec(memory_space=pl.ANY)
    held = pl.BlockSpec(memory_space=pltpu.VMEM)
    return pl.pallas_call(
        lambda *refs: pair_kernel(factor, steps, *refs),
        in_specs=[SCALAR, free, free, free],
        out_specs=[held, held, free],
        out_shape=[
            jax.ShapeDtypeStruct((clips, features), F32),
            jax.ShapeDtypeStruct((clips, features), BF16),
            jax.ShapeDtypeStruct((rows, features), BF16),
        ],
        scratch_shapes=[
            pltpu.VMEM((rows, features), BF16),
            pltpu.VMEM((2 * clips, features), BF16),
            pltpu.VMEM((rows, features), BF16),
            pltpu.VMEM((2 * clips, features), F32),
            pltpu.SemaphoreType.DMA((2 + steps,)),
            pltpu.SemaphoreType.DMA((steps,)),
        ],
        compiler_params=ALL_ROOM,
        cost_estimate=pl.CostEstimate(
            flops=12 * rows * clips * features, bytes_accessed=5 * rows * features, transcendentals=0
        ),
    )(place, line, own, mate)


def clip_kernel(kept_ref, arrived_ref, slope_ref, place_ref, stay_ref, give_ref):
    grad = (kept_ref[...] + arrived_ref[...].astype(F32)).astype(BF16)
    slots, clips = stay_ref.shape[0], grad.shape[0]
    slot = lax.broadcasted_iota(jnp.int32, (slots, clips), 0)
    stay_ref[...] = dot_of((slot == place_ref[...]).astype(BF16), grad, 1, 0).astype(BF16)
    other = dot_of((slot + slots == place_ref[...]).astype(BF16), grad, 1, 0)
    give_ref[pl.ds(0, slots)] = other.astype(BF16)
    give_ref[pl.ds(slots, clips)] = (grad.astype(F32) * slope_ref[...]).astype(BF16)


def clip_grads(kept, arrived, slope, places, slots):
    clips, features = kept.shape
    return pl.pallas_call(
        clip_kernel,
        out_shape=[
            jax.ShapeDtypeStruct((slots // 2, features), BF16),
            jax.ShapeDtypeStruct((slots // 2 + clips, features), BF16),
        ],
        compiler_params=ROOM,
    )(kept, arrived, slope, places[None, :])


def merge_kernel(core_ref, stay_ref, got_ref, out_ref):
    count, lines, features = out_ref.shape
    shape = (count, lines // 2, features)
    stay = stay_ref[...].astype(F32).reshape(shape)
    got = got_ref[pl.ds(0, stay_ref.shape[0])].astype(F32).reshape(shape)
    first = core_ref[0] == 0
    pair = [jnp.where(first, stay, got), jnp.where(first, got, stay)]
    out_ref[...] = jnp.concatenate(pair, axis=1).astype(BF16)


def merged(stay, got, core, count):
    rows, features = stay.shape
    held = pl.BlockSpec(memory_space=pltpu.VMEM)
    return pl.pallas_call(
        merge_kernel,
        in_specs=[SCALAR, held, held],
        out_specs=held,
        out_shape=jax.ShapeDtypeStruct((count, 2 * rows // count, features), BF16),
        compiler_params=ROOM,
    )(core, stay, got)


def weight_kernel(own_picked, mate_picked, own_ref, mate_ref, *out_refs):
    share = out_refs[0].shape[0]
    clips = own_picked.shape[0]
    rows = pl.ds(own_ref.shape[0] - clips, clips)
    picked = jnp.concatenate([own_picked[...], mate_picked[...]], axis=0)
    pre = jnp.concatenate([own_ref[rows], mate_ref[rows]], axis=0)
    product = dot_of(picked, pre, 0, 0)
    for d, out_ref in enumerate(out_refs):
        out_ref[...] = product[d * share : (d + 1) * share].astype(out_ref.dtype)


def weight_parts(own_picked, mate_picked, own, mate, count):
    half, features = own_picked.shape[1], own.shape[1]
    shape = (half // count, features)
    return pl.pallas_call(
        weight_kernel,
        out_shape=[jax.ShapeDtypeStruct(shape, F32 if d == 0 else BF16) for d in range(count)],
        compiler_params=ROOM,
    )(own_picked, mate_picked, own, mate)


def shards(audio, video, owner, clip_feats, lengths, proj_weight):
    clips, features = audio.shape
    blocks = lax.axis_size(BLK)
    core = lax.axis_index("wide_c")
    place = lax.axis_index("blk_z").astype(jnp.int32)[None]
    audio_line = lax.all_gather(audio, "blk_z", axis=0, tiled=True)

    peers = lax.axis_size(WIDE)
    slots = clip_feats.shape[0]
    capacity = slots // peers
    length_scale = lax.rsqrt(lengths.astype(F32))[:, None]
    pooled = (clip_feats.astype(F32) * length_scale).astype(BF16)
    pooled_slots = lax.all_to_all(
        pooled.reshape(peers, capacity, features), WIDE, 0, 0, tiled=True
    ).reshape(slots, features)
    video_mate = swapped(video, "blk_x")
    slope_own = gelu_slope(dot_of(pooled, proj_weight, 1, 0))

    peer = owner[:, 0]
    ranks = ranks_of(peer)
    slot_of = peer * capacity + ranks
    placing = (slot_of[:, None] == jnp.arange(slots, dtype=jnp.int32)[None, :]).astype(BF16)
    places = (((peer % 2) ^ core) * (peers // 2) + peer // 2) * capacity + ranks
    clip_rows = dot_of(placing, pooled_slots, 1, 0).astype(BF16)
    slope_rows = gelu_slope(dot_of(clip_rows, proj_weight, 1, 0))
    picked = dot_of(clip_rows, picking_of(core, features), 1, 0).astype(BF16)
    picked_mate = swapped(
        dot_of(clip_rows, picking_of(1 - core, features), 1, 0).astype(BF16), "wide_c"
    )
    audio_line, video_mate, slope_rows, picked, picked_mate, slope_own, places = (
        lax.optimization_barrier(
            (audio_line, video_mate, slope_rows, picked, picked_mate, slope_own, places)
        )
    )

    kept, sent, line_grads = pair_grads(audio_line, video, video_mate, place, 4.0 / blocks, 4)
    audio_grad = lax.psum_scatter(line_grads, "blk_z", scatter_dimension=0, tiled=True)
    arrived = swapped(sent, "blk_x")
    stay, give = clip_grads(kept, arrived, slope_rows, places, slots)
    got = swapped(give, "wide_c")
    packed = merged(stay, got, core.astype(jnp.int32)[None], peers // 2)
    received = lax.all_to_all(packed, ("wide_y", "wide_x"), 0, 0, tiled=True)
    received = received.reshape(slots, features)

    parts = weight_parts(picked, picked_mate, give, got, 4)
    summed = parts[0]
    for d in (2, 1, 3):
        pairs = [(at, at ^ d) for at in range(4)]
        summed = summed + lax.ppermute(parts[d], ("wide_x", "blk_x"), pairs).astype(F32)
    summed = summed.astype(BF16)
    summed, received = lax.optimization_barrier((summed, received))
    ny = lax.axis_size("wide_y")
    pieces = lax.all_to_all(summed.reshape(ny, -1, features), "wide_y", 0, 0, tiled=True)
    pre_grad = (received.astype(F32) * slope_own).astype(BF16)
    feats_grad = (dot_of(pre_grad, proj_weight, 1, 1) * length_scale).astype(BF16)
    pieces, feats_grad = lax.optimization_barrier((pieces, feats_grad))
    total = jnp.sum(pieces.astype(F32), axis=0).astype(BF16)
    gathered = lax.all_to_all(
        jnp.broadcast_to(total[None], (blocks, *total.shape)), BLK, 0, 0, tiled=True
    )
    gathered = gathered.reshape(lax.axis_size("blk_x"), -1, *total.shape)
    weight_grad = jnp.sum(gathered.astype(F32), axis=1).reshape(-1, features)
    return (audio_grad, feats_grad, weight_grad)


def solution(mesh):
    finer = Mesh(mesh.devices.reshape(8, 2, 2, 2, 8), AXES)
    rows = P(AXES, None)
    return jax.shard_map(
        shards,
        mesh=finer,
        in_specs=(rows, rows, rows, rows, P(AXES), P()),
        out_specs=(rows, rows, P(WIDE, None)),
        check_vma=False,
    )
```

```python
import jax
import jax.numpy as jnp
from jax import lax
from jax.experimental import pallas as pl
from jax.experimental.pallas import tpu as pltpu
from jax.sharding import Mesh
from jax.sharding import PartitionSpec as P

AXES = ("wide_y", "wide_x", "wide_c", "blk_x", "blk_z")
WIDE = ("wide_y", "wide_x", "wide_c")
BLK = ("blk_x", "blk_z")
BF16 = jnp.bfloat16
F32 = jnp.float32
ROOM = pltpu.CompilerParams(vmem_limit_bytes=24 * 2**20)
ALL_ROOM = pltpu.CompilerParams(vmem_limit_bytes=56 * 2**20)
SCALAR = pl.BlockSpec(memory_space=pltpu.SMEM)


def swapped(array, axis):
    return lax.ppermute(array, axis, [(0, 1), (1, 0)])


def dot_of(matrix_a, matrix_b, dim_a, dim_b):
    return lax.dot_general(
        matrix_a, matrix_b, (((dim_a,), (dim_b,)), ((), ())), preferred_element_type=F32
    )


def gelu_slope(v):
    cdf = 0.5 * (1.0 + lax.erf(v * 0.7071067811865476))
    return cdf + v * (0.3989422804014327 * jnp.exp(-0.5 * v * v))


def ranks_of(peer):
    ids = jnp.arange(peer.shape[0], dtype=jnp.int32)
    before = (peer[:, None] == peer[None, :]) & (ids[:, None] < ids[None, :])
    return jnp.sum(before.astype(jnp.int32), axis=0)


def picking_of(core, feature_count):
    half = feature_count // 2
    ny, nx = lax.axis_size("wide_y"), lax.axis_size("wide_x")
    bx = lax.axis_size("blk_x")
    share = half // (ny * nx * bx)
    place = jnp.arange(half, dtype=jnp.int32)
    within, rest = place % share, place // share
    owner, line = rest % (ny * nx), (rest // (ny * nx)) ^ lax.axis_index("blk_x")
    feature = ((owner * 2 + core) * bx + line) * share + within
    return (jnp.arange(feature_count, dtype=jnp.int32)[:, None] == feature[None, :]).astype(BF16)


def pair_kernel(factor, steps, place_ref, line_hbm, own_hbm, mate_hbm, slope_hbm,
                kept_ref, sent_ref, pre_ref, grads_hbm, line, video, slope, grads, total, came, gone):
    rows, clips = line.shape[0] // steps, own_hbm.shape[0]
    loads = [
        pltpu.make_async_copy(own_hbm, video.at[pl.ds(0, clips)], came.at[0]),
        pltpu.make_async_copy(mate_hbm, video.at[pl.ds(clips, clips)], came.at[1]),
    ]
    for step in range(steps):
        block = pl.ds(step * rows, rows)
        loads.append(pltpu.make_async_copy(line_hbm.at[block], line.at[block], came.at[2 + step]))
    loads.append(pltpu.make_async_copy(slope_hbm, slope, came.at[2 + steps]))
    for load in loads:
        load.start()
    loads[0].wait()
    loads[1].wait()

    def coeffs_of(step):
        block = pl.ds(step * rows, rows)
        loads[2 + step].wait()
        scores = dot_of(video[...], line[block], 1, 1)
        row = lax.broadcasted_iota(jnp.int32, scores.shape, 0)
        col = lax.broadcasted_iota(jnp.int32, scores.shape, 1) + step * rows
        labels = ((col == place_ref[0] * clips + row) & (row < clips)).astype(F32)
        return (factor * (jax.nn.sigmoid(4.0 * scores - 2.0) - labels)).astype(BF16)

    stores = []
    coeffs = coeffs_of(0)
    for step in range(steps):
        block = pl.ds(step * rows, rows)
        ready = coeffs
        if step + 1 < steps:
            coeffs = coeffs_of(step + 1)
        part = dot_of(ready, line[block], 1, 0)
        if step == 0:
            total[...] = part
        else:
            total[...] += part
        grads[block] = dot_of(ready, video[...], 0, 0).astype(BF16)
        stores.append(pltpu.make_async_copy(grads.at[block], grads_hbm.at[block], gone.at[step]))
        stores[-1].start()
    loads[-1].wait()
    kept_ref[...] = total[:clips]
    sent_ref[...] = total[clips:].astype(BF16)
    pre_ref[...] = (total[...] * slope[...]).astype(BF16)
    for store in stores:
        store.wait()


def pair_grads(line, own, mate, slope, place, factor, steps):
    rows, features = line.shape
    clips = own.shape[0]
    free = pl.BlockSpec(memory_space=pl.ANY)
    held = pl.BlockSpec(memory_space=pltpu.VMEM)
    return pl.pallas_call(
        lambda *refs: pair_kernel(factor, steps, *refs),
        in_specs=[SCALAR, free, free, free, free],
        out_specs=[held, held, held, free],
        out_shape=[
            jax.ShapeDtypeStruct((clips, features), F32),
            jax.ShapeDtypeStruct((clips, features), BF16),
            jax.ShapeDtypeStruct((2 * clips, features), BF16),
            jax.ShapeDtypeStruct((rows, features), BF16),
        ],
        scratch_shapes=[
            pltpu.VMEM((rows, features), BF16),
            pltpu.VMEM((2 * clips, features), BF16),
            pltpu.VMEM((2 * clips, features), F32),
            pltpu.VMEM((rows, features), BF16),
            pltpu.VMEM((2 * clips, features), F32),
            pltpu.SemaphoreType.DMA((3 + steps,)),
            pltpu.SemaphoreType.DMA((steps,)),
        ],
        compiler_params=ALL_ROOM,
        cost_estimate=pl.CostEstimate(
            flops=12 * rows * clips * features, bytes_accessed=5 * rows * features, transcendentals=0
        ),
    )(place, line, own, mate, slope)


def clip_kernel(kept_ref, arrived_ref, place_ref, stay_ref, give_ref):
    grad = (kept_ref[...] + arrived_ref[...].astype(F32)).astype(BF16)
    slots, clips = stay_ref.shape[0], grad.shape[0]
    slot = lax.broadcasted_iota(jnp.int32, (slots, clips), 0)
    stay_ref[...] = dot_of((slot == place_ref[...]).astype(BF16), grad, 1, 0).astype(BF16)
    give_ref[...] = dot_of((slot + slots == place_ref[...]).astype(BF16), grad, 1, 0).astype(BF16)


def clip_grads(kept, arrived, places, slots):
    shape = jax.ShapeDtypeStruct((slots // 2, kept.shape[1]), BF16)
    return pl.pallas_call(
        clip_kernel,
        out_shape=[shape, shape],
        compiler_params=ROOM,
    )(kept, arrived, places[None, :])


def weight_kernel(own_picked, mate_picked, own_pre, mate_pre, keep_ref, give_ref):
    half = keep_ref.shape[0]
    for at, out_ref in ((half, give_ref), (0, keep_ref)):
        block = pl.ds(at, half)
        product = dot_of(own_picked[block], own_pre[...], 1, 0)
        product += dot_of(mate_picked[block], mate_pre[...], 1, 0)
        out_ref[...] = product.astype(out_ref.dtype)


def weight_parts(own_picked, mate_picked, own_pre, mate_pre):
    shape = (own_picked.shape[0] // 2, own_pre.shape[1])
    return pl.pallas_call(
        weight_kernel,
        out_shape=[jax.ShapeDtypeStruct(shape, F32), jax.ShapeDtypeStruct(shape, BF16)],
        compiler_params=ROOM,
    )(own_picked, mate_picked, own_pre, mate_pre)


def load_kernel(core_ref, stay_ref, got_ref, keep_ref, came_ref, out_ref):
    count, lines, features = out_ref.shape
    cells = stay_ref.shape[0] // count
    stay = stay_ref[...].astype(F32).reshape(count, cells, features)
    got = got_ref[...].astype(F32).reshape(count, cells, features)
    first = core_ref[0] == 0
    pair = [jnp.where(first, stay, got), jnp.where(first, got, stay)]
    out_ref[:, pl.ds(0, 2 * cells)] = jnp.concatenate(pair, axis=1).astype(BF16)
    rows = lines - 2 * cells
    total = (keep_ref[...] + came_ref[...].astype(F32)).reshape(count, rows, features)
    out_ref[:, pl.ds(2 * cells, rows)] = total.astype(BF16)


def load_of(core, stay, got, keep, came, count):
    lines = (2 * stay.shape[0] + keep.shape[0]) // count
    held = pl.BlockSpec(memory_space=pltpu.VMEM)
    return pl.pallas_call(
        load_kernel,
        in_specs=[SCALAR, held, held, held, held],
        out_specs=held,
        out_shape=jax.ShapeDtypeStruct((count, lines, stay.shape[1]), BF16),
        compiler_params=ROOM,
    )(core, stay, got, keep, came)


def spread_kernel(pieces_ref, out_ref):
    total = pieces_ref[0].astype(F32)
    for s in range(1, pieces_ref.shape[0]):
        total += pieces_ref[s].astype(F32)
    out_ref[...] = jnp.broadcast_to(total.astype(BF16)[None], out_ref.shape)


def sum_spread(pieces, rows, copies):
    count, lines, features = pieces.shape
    return pl.pallas_call(
        spread_kernel,
        grid=(1,),
        in_specs=[pl.BlockSpec((count, rows, features), lambda i: (0, lines // rows - 1, 0))],
        out_specs=pl.BlockSpec((copies, rows, features), lambda i: (0, 0, 0)),
        out_shape=jax.ShapeDtypeStruct((copies, rows, features), BF16),
        compiler_params=ROOM,
    )(pieces)


def shards(audio, video, owner, clip_feats, lengths, proj_weight):
    clips, features = audio.shape
    blocks = lax.axis_size(BLK)
    core = lax.axis_index("wide_c")
    place = lax.axis_index("blk_z").astype(jnp.int32)[None]
    audio_line = lax.all_gather(audio, "blk_z", axis=0, tiled=True)

    peers = lax.axis_size(WIDE)
    slots = clip_feats.shape[0]
    capacity = slots // peers
    length_scale = lax.rsqrt(lengths.astype(F32))[:, None]
    pooled = (clip_feats.astype(F32) * length_scale).astype(BF16)
    pooled_slots = lax.all_to_all(
        pooled.reshape(peers, capacity, features), WIDE, 0, 0, tiled=True
    ).reshape(slots, features)
    video_mate = swapped(video, "blk_x")
    slope_own = gelu_slope(dot_of(pooled, proj_weight, 1, 0))

    peer = owner[:, 0]
    ranks = ranks_of(peer)
    slot_of = peer * capacity + ranks
    placing = (slot_of[:, None] == jnp.arange(slots, dtype=jnp.int32)[None, :]).astype(BF16)
    places = (((peer % 2) ^ core) * (peers // 2) + peer // 2) * capacity + ranks
    clip_rows = dot_of(placing, pooled_slots, 1, 0).astype(BF16)
    row_pair = jnp.concatenate([clip_rows, swapped(clip_rows, "blk_x")])
    slope_pair = gelu_slope(dot_of(row_pair, proj_weight, 1, 0))
    picked = dot_of(picking_of(core, features), row_pair, 0, 1).astype(BF16)
    picked_mate = swapped(
        dot_of(picking_of(1 - core, features), row_pair, 0, 1).astype(BF16), "wide_c"
    )
    audio_line, video_mate, slope_pair, picked, picked_mate, slope_own, places = (
        lax.optimization_barrier(
            (audio_line, video_mate, slope_pair, picked, picked_mate, slope_own, places)
        )
    )

    kept, sent, pre_pair, line_grads = pair_grads(
        audio_line, video, video_mate, slope_pair, place, 4.0 / blocks, 4
    )
    audio_grad = lax.psum_scatter(line_grads, "blk_z", scatter_dimension=0, tiled=True)

    pre_mate = swapped(pre_pair, "wide_c")
    arrived = swapped(sent, "blk_x")
    keep, other_line = weight_parts(picked, picked_mate, pre_pair, pre_mate)
    came = swapped(other_line, "blk_x")

    arrived, other_line = lax.optimization_barrier((arrived, other_line))
    stay, give = clip_grads(kept, arrived, places, slots)
    got = swapped(give, "wide_c")
    load = load_of(core.astype(jnp.int32)[None], stay, got, keep, came, peers // 2)
    rows = keep.shape[0] // (peers // 2)
    load = lax.all_to_all(load, ("wide_y", "wide_x"), 0, 0, tiled=True)

    total = sum_spread(load, rows, blocks)
    gathered = lax.all_to_all(total, BLK, 0, 0, tiled=True)
    received = load[:, :-rows].reshape(slots, features)
    pre_grad = (received.astype(F32) * slope_own).astype(BF16)
    feats_grad = (dot_of(pre_grad, proj_weight, 1, 1) * length_scale).astype(BF16)
    gathered, feats_grad = lax.optimization_barrier((gathered, feats_grad))
    gathered = gathered.reshape(lax.axis_size("blk_x"), -1, *total.shape[1:])
    weight_grad = jnp.sum(gathered.astype(F32), axis=1).reshape(-1, features)
    return (audio_grad, feats_grad, weight_grad)


def solution(mesh):
    finer = Mesh(mesh.devices.reshape(8, 2, 2, 2, 8), AXES)
    rows = P(AXES, None)
    return jax.shard_map(
        shards,
        mesh=finer,
        in_specs=(rows, rows, rows, rows, P(AXES), P()),
        out_specs=(rows, rows, P(WIDE, None)),
        check_vma=False,
    )
```

```python
import jax
import jax.numpy as jnp
from jax import lax
from jax.experimental import pallas as pl
from jax.experimental.pallas import tpu as pltpu
from jax.sharding import Mesh
from jax.sharding import PartitionSpec as P

AXES = ("wide_y", "wide_x", "wide_c", "blk_x", "blk_z")
WIDE = ("wide_y", "wide_x", "wide_c")
BLK = ("blk_x", "blk_z")
BF16 = jnp.bfloat16
F32 = jnp.float32
ROOM = pltpu.CompilerParams(vmem_limit_bytes=24 * 2**20)
ALL_ROOM = pltpu.CompilerParams(vmem_limit_bytes=56 * 2**20)
SCALAR = pl.BlockSpec(memory_space=pltpu.SMEM)


def swapped(array, axis):
    return lax.ppermute(array, axis, [(0, 1), (1, 0)])


def dot_of(matrix_a, matrix_b, dim_a, dim_b):
    return lax.dot_general(
        matrix_a, matrix_b, (((dim_a,), (dim_b,)), ((), ())), preferred_element_type=F32
    )


def gelu_slope(v):
    cdf = 0.5 * (1.0 + lax.erf(v * 0.7071067811865476))
    return cdf + v * (0.3989422804014327 * jnp.exp(-0.5 * v * v))


def targets_of(owner, capacity):
    ids = jnp.arange(owner.shape[0], dtype=jnp.int32)
    peer = owner[:, 0]
    before = (peer[:, None] == peer[None, :]) & (ids[:, None] < ids[None, :])
    return peer * capacity + jnp.sum(before.astype(jnp.int32), axis=0)


def picking_of(core, feature_count):
    half = feature_count // 2
    ny, nx = lax.axis_size("wide_y"), lax.axis_size("wide_x")
    bx = lax.axis_size("blk_x")
    share = half // (ny * nx * bx)
    place = jnp.arange(half, dtype=jnp.int32)
    within, rest = place % share, place // share
    y, apart = rest % ny, rest // ny
    x_wide = (apart // bx) ^ lax.axis_index("wide_x")
    x_blk = (apart % bx) ^ lax.axis_index("blk_x")
    feature = (((y * nx + x_wide) * 2 + core) * bx + x_blk) * share + within
    return (jnp.arange(feature_count, dtype=jnp.int32)[:, None] == feature[None, :]).astype(BF16)


def pair_kernel(factor, steps, place_ref, line_hbm, own_hbm, mate_hbm,
                kept_ref, sent_ref, grads_hbm, line, video, grads, total, came, gone):
    rows, clips = line.shape[0] // steps, own_hbm.shape[0]
    loads = [
        pltpu.make_async_copy(own_hbm, video.at[pl.ds(0, clips)], came.at[0]),
        pltpu.make_async_copy(mate_hbm, video.at[pl.ds(clips, clips)], came.at[1]),
    ]
    for step in range(steps):
        block = pl.ds(step * rows, rows)
        loads.append(pltpu.make_async_copy(line_hbm.at[block], line.at[block], came.at[2 + step]))
    for load in loads:
        load.start()
    loads[0].wait()
    loads[1].wait()

    def coeffs_of(step):
        block = pl.ds(step * rows, rows)
        loads[2 + step].wait()
        scores = dot_of(video[...], line[block], 1, 1)
        row = lax.broadcasted_iota(jnp.int32, scores.shape, 0)
        col = lax.broadcasted_iota(jnp.int32, scores.shape, 1) + step * rows
        labels = ((col == place_ref[0] * clips + row) & (row < clips)).astype(F32)
        return (factor * (jax.nn.sigmoid(4.0 * scores - 2.0) - labels)).astype(BF16)

    stores = []
    coeffs = coeffs_of(0)
    for step in range(steps):
        block = pl.ds(step * rows, rows)
        ready = coeffs
        if step + 1 < steps:
            coeffs = coeffs_of(step + 1)
        part = dot_of(ready, line[block], 1, 0)
        if step == 0:
            total[...] = part
        else:
            total[...] += part
        grads[block] = dot_of(ready, video[...], 0, 0).astype(BF16)
        stores.append(pltpu.make_async_copy(grads.at[block], grads_hbm.at[block], gone.at[step]))
        stores[-1].start()
    kept_ref[...] = total[:clips]
    sent_ref[...] = total[clips:].astype(BF16)
    for store in stores:
        store.wait()


def pair_grads(line, own, mate, place, factor, steps):
    rows, features = line.shape
    clips = own.shape[0]
    free = pl.BlockSpec(memory_space=pl.ANY)
    held = pl.BlockSpec(memory_space=pltpu.VMEM)
    return pl.pallas_call(
        lambda *refs: pair_kernel(factor, steps, *refs),
        in_specs=[SCALAR, free, free, free],
        out_specs=[held, held, free],
        out_shape=[
            jax.ShapeDtypeStruct((clips, features), F32),
            jax.ShapeDtypeStruct((clips, features), BF16),
            jax.ShapeDtypeStruct((rows, features), BF16),
        ],
        scratch_shapes=[
            pltpu.VMEM((rows, features), BF16),
            pltpu.VMEM((2 * clips, features), BF16),
            pltpu.VMEM((rows, features), BF16),
            pltpu.VMEM((2 * clips, features), F32),
            pltpu.SemaphoreType.DMA((2 + steps,)),
            pltpu.SemaphoreType.DMA((steps,)),
        ],
        compiler_params=ALL_ROOM,
        cost_estimate=pl.CostEstimate(
            flops=12 * rows * clips * features, bytes_accessed=5 * rows * features, transcendentals=0
        ),
    )(place, line, own, mate)


def clip_kernel(kept_ref, arrived_ref, target_ref, packed_ref):
    grad = (kept_ref[...] + arrived_ref[...].astype(F32)).astype(BF16)
    slots, clips = packed_ref.shape[0], grad.shape[0]
    slot = lax.broadcasted_iota(jnp.int32, (slots, clips), 0)
    placing = (slot == target_ref[...]).astype(BF16)
    packed_ref[...] = dot_of(placing, grad, 1, 0).astype(BF16)


def clip_grads(kept, arrived, targets, slots):
    return pl.pallas_call(
        clip_kernel,
        out_shape=jax.ShapeDtypeStruct((slots, kept.shape[1]), BF16),
        compiler_params=ROOM,
    )(kept, arrived, targets[None, :])


def product_kernel(kept_ref, arrived_ref, slope_ref, pre_ref):
    grad = (kept_ref[...] + arrived_ref[...].astype(F32)).astype(BF16)
    pre_ref[...] = (grad.astype(F32) * slope_ref[...]).astype(BF16)


def product_rows(kept, arrived, slope):
    return pl.pallas_call(
        product_kernel,
        out_shape=jax.ShapeDtypeStruct(kept.shape, BF16),
        compiler_params=ROOM,
    )(kept, arrived, slope)


def weight_kernel(own_picked, mate_picked, own_pre, mate_pre, *out_refs):
    share = out_refs[0].shape[0]
    picked = jnp.concatenate([own_picked[...], mate_picked[...]], axis=0)
    pre = jnp.concatenate([own_pre[...], mate_pre[...]], axis=0)
    product = dot_of(picked, pre, 0, 0)
    for d, out_ref in enumerate(out_refs):
        out_ref[...] = product[d * share : (d + 1) * share].astype(out_ref.dtype)


def weight_parts(own_picked, mate_picked, own_pre, mate_pre, count):
    half, features = own_picked.shape[1], own_pre.shape[1]
    shape = (half // count, features)
    return pl.pallas_call(
        weight_kernel,
        out_shape=[jax.ShapeDtypeStruct(shape, F32 if d == 0 else BF16) for d in range(count)],
        compiler_params=ROOM,
    )(own_picked, mate_picked, own_pre, mate_pre)


def shards(audio, video, owner, clip_feats, lengths, proj_weight):
    clips, features = audio.shape
    blocks = lax.axis_size(BLK)
    core = lax.axis_index("wide_c")
    place = lax.axis_index("blk_z").astype(jnp.int32)[None]
    audio_line = lax.all_gather(audio, "blk_z", axis=0, tiled=True)

    peers = lax.axis_size(WIDE)
    slots = clip_feats.shape[0]
    capacity = slots // peers
    length_scale = lax.rsqrt(lengths.astype(F32))[:, None]
    pooled = (clip_feats.astype(F32) * length_scale).astype(BF16)
    pooled_slots = lax.all_to_all(
        pooled.reshape(peers, capacity, features), WIDE, 0, 0, tiled=True
    ).reshape(slots, features)
    video_mate = swapped(video, "blk_x")
    slope_own = gelu_slope(dot_of(pooled, proj_weight, 1, 0))

    targets = targets_of(owner, capacity)
    placing = (targets[:, None] == jnp.arange(slots, dtype=jnp.int32)[None, :]).astype(BF16)
    clip_rows = dot_of(placing, pooled_slots, 1, 0).astype(BF16)
    slope_rows = gelu_slope(dot_of(clip_rows, proj_weight, 1, 0))
    picked = dot_of(clip_rows, picking_of(core, features), 1, 0).astype(BF16)
    picked_mate = swapped(
        dot_of(clip_rows, picking_of(1 - core, features), 1, 0).astype(BF16), "wide_c"
    )
    audio_line, video_mate, slope_rows, picked, picked_mate, slope_own, targets = (
        lax.optimization_barrier(
            (audio_line, video_mate, slope_rows, picked, picked_mate, slope_own, targets)
        )
    )

    kept, sent, line_grads = pair_grads(audio_line, video, video_mate, place, 4.0 / blocks, 4)
    audio_grad = lax.psum_scatter(line_grads, "blk_z", scatter_dimension=0, tiled=True)
    arrived = swapped(sent, "blk_x")
    packed = clip_grads(kept, arrived, targets, slots)
    pre_rows = product_rows(kept, arrived, slope_rows)
    received = lax.all_to_all(
        packed.reshape(peers, capacity, features), WIDE, 0, 0, tiled=True
    ).reshape(slots, features)

    pre_mate = swapped(pre_rows, "wide_c")
    parts = weight_parts(picked, picked_mate, pre_rows, pre_mate, 4)
    summed = parts[0]
    for d in (2, 1, 3):
        pairs = [(at, at ^ d) for at in range(4)]
        summed = summed + lax.ppermute(parts[d], ("wide_x", "blk_x"), pairs).astype(F32)
    summed = summed.astype(BF16)
    summed, received = lax.optimization_barrier((summed, received))
    ny = lax.axis_size("wide_y")
    pieces = lax.all_to_all(summed.reshape(ny, -1, features), "wide_y", 0, 0, tiled=True)
    pre_grad = (received.astype(F32) * slope_own).astype(BF16)
    feats_grad = (dot_of(pre_grad, proj_weight, 1, 1) * length_scale).astype(BF16)
    pieces, feats_grad = lax.optimization_barrier((pieces, feats_grad))
    total = jnp.sum(pieces.astype(F32), axis=0).astype(BF16)
    gathered = lax.all_to_all(
        jnp.broadcast_to(total[None], (blocks, *total.shape)), BLK, 0, 0, tiled=True
    )
    gathered = gathered.reshape(lax.axis_size("blk_x"), -1, *total.shape)
    weight_grad = jnp.sum(gathered.astype(F32), axis=1).reshape(-1, features)
    return (audio_grad, feats_grad, weight_grad)


def solution(mesh):
    finer = Mesh(mesh.devices.reshape(8, 2, 2, 2, 8), AXES)
    rows = P(AXES, None)
    return jax.shard_map(
        shards,
        mesh=finer,
        in_specs=(rows, rows, rows, rows, P(AXES), P()),
        out_specs=(rows, rows, P(WIDE, None)),
        check_vma=False,
    )
```

```python
import jax
import jax.numpy as jnp
from jax import lax
from jax.experimental import pallas as pl
from jax.experimental.pallas import tpu as pltpu
from jax.sharding import Mesh
from jax.sharding import PartitionSpec as P

AXES = ("wide_y", "wide_x", "wide_c", "blk_x", "blk_z")
WIDE = ("wide_y", "wide_x", "wide_c")
BLK = ("blk_x", "blk_z")
BF16 = jnp.bfloat16
F32 = jnp.float32
ROOM = pltpu.CompilerParams(vmem_limit_bytes=24 * 2**20)
ALL_ROOM = pltpu.CompilerParams(vmem_limit_bytes=56 * 2**20)
SCALAR = pl.BlockSpec(memory_space=pltpu.SMEM)


def swapped(array, axis):
    return lax.ppermute(array, axis, [(0, 1), (1, 0)])


def dot_of(matrix_a, matrix_b, dim_a, dim_b):
    return lax.dot_general(
        matrix_a, matrix_b, (((dim_a,), (dim_b,)), ((), ())), preferred_element_type=F32
    )


def gelu_slope(v):
    cdf = 0.5 * (1.0 + lax.erf(v * 0.7071067811865476))
    return cdf + v * (0.3989422804014327 * jnp.exp(-0.5 * v * v))


def targets_of(owner, capacity):
    ids = jnp.arange(owner.shape[0], dtype=jnp.int32)
    peer = owner[:, 0]
    before = (peer[:, None] == peer[None, :]) & (ids[:, None] < ids[None, :])
    return peer * capacity + jnp.sum(before.astype(jnp.int32), axis=0)


def picking_of(core, feature_count):
    half = feature_count // 2
    ny, nx = lax.axis_size("wide_y"), lax.axis_size("wide_x")
    bx = lax.axis_size("blk_x")
    share = half // (ny * nx * bx)
    place = jnp.arange(half, dtype=jnp.int32)
    within, rest = place % share, place // share
    owner, line = rest % (ny * nx), (rest // (ny * nx)) ^ lax.axis_index("blk_x")
    feature = ((owner * 2 + core) * bx + line) * share + within
    return (jnp.arange(feature_count, dtype=jnp.int32)[:, None] == feature[None, :]).astype(BF16)


def pair_kernel(factor, steps, place_ref, line_hbm, own_hbm, mate_hbm,
                kept_ref, sent_ref, grads_hbm, line, video, grads, total, came, gone):
    rows, clips = line.shape[0] // steps, own_hbm.shape[0]
    loads = [
        pltpu.make_async_copy(own_hbm, video.at[pl.ds(0, clips)], came.at[0]),
        pltpu.make_async_copy(mate_hbm, video.at[pl.ds(clips, clips)], came.at[1]),
    ]
    for step in range(steps):
        block = pl.ds(step * rows, rows)
        loads.append(pltpu.make_async_copy(line_hbm.at[block], line.at[block], came.at[2 + step]))
    for load in loads:
        load.start()
    loads[0].wait()
    loads[1].wait()

    def coeffs_of(step):
        block = pl.ds(step * rows, rows)
        loads[2 + step].wait()
        scores = dot_of(video[...], line[block], 1, 1)
        row = lax.broadcasted_iota(jnp.int32, scores.shape, 0)
        col = lax.broadcasted_iota(jnp.int32, scores.shape, 1) + step * rows
        labels = ((col == place_ref[0] * clips + row) & (row < clips)).astype(F32)
        return (factor * (jax.nn.sigmoid(4.0 * scores - 2.0) - labels)).astype(BF16)

    stores = []
    coeffs = coeffs_of(0)
    for step in range(steps):
        block = pl.ds(step * rows, rows)
        ready = coeffs
        if step + 1 < steps:
            coeffs = coeffs_of(step + 1)
        part = dot_of(ready, line[block], 1, 0)
        if step == 0:
            total[...] = part
        else:
            total[...] += part
        grads[block] = dot_of(ready, video[...], 0, 0).astype(BF16)
        stores.append(pltpu.make_async_copy(grads.at[block], grads_hbm.at[block], gone.at[step]))
        stores[-1].start()
    kept_ref[...] = total[:clips]
    sent_ref[...] = total[clips:].astype(BF16)
    for store in stores:
        store.wait()


def pair_grads(line, own, mate, place, factor, steps):
    rows, features = line.shape
    clips = own.shape[0]
    free = pl.BlockSpec(memory_space=pl.ANY)
    held = pl.BlockSpec(memory_space=pltpu.VMEM)
    return pl.pallas_call(
        lambda *refs: pair_kernel(factor, steps, *refs),
        in_specs=[SCALAR, free, free, free],
        out_specs=[held, held, free],
        out_shape=[
            jax.ShapeDtypeStruct((clips, features), F32),
            jax.ShapeDtypeStruct((clips, features), BF16),
            jax.ShapeDtypeStruct((rows, features), BF16),
        ],
        scratch_shapes=[
            pltpu.VMEM((rows, features), BF16),
            pltpu.VMEM((2 * clips, features), BF16),
            pltpu.VMEM((rows, features), BF16),
            pltpu.VMEM((2 * clips, features), F32),
            pltpu.SemaphoreType.DMA((2 + steps,)),
            pltpu.SemaphoreType.DMA((steps,)),
        ],
        compiler_params=ALL_ROOM,
        cost_estimate=pl.CostEstimate(
            flops=12 * rows * clips * features, bytes_accessed=5 * rows * features, transcendentals=0
        ),
    )(place, line, own, mate)


def clip_kernel(kept_ref, arrived_ref, target_ref, packed_ref):
    grad = (kept_ref[...] + arrived_ref[...].astype(F32)).astype(BF16)
    slots, clips = packed_ref.shape[0], grad.shape[0]
    slot = lax.broadcasted_iota(jnp.int32, (slots, clips), 0)
    placing = (slot == target_ref[...]).astype(BF16)
    packed_ref[...] = dot_of(placing, grad, 1, 0).astype(BF16)


def clip_grads(kept, arrived, targets, slots):
    return pl.pallas_call(
        clip_kernel,
        out_shape=jax.ShapeDtypeStruct((slots, kept.shape[1]), BF16),
        compiler_params=ROOM,
    )(kept, arrived, targets[None, :])


def product_kernel(kept_ref, arrived_ref, slope_ref, pre_ref):
    grad = (kept_ref[...] + arrived_ref[...].astype(F32)).astype(BF16)
    pre_ref[...] = (grad.astype(F32) * slope_ref[...]).astype(BF16)


def product_rows(kept, arrived, slope):
    return pl.pallas_call(
        product_kernel,
        out_shape=jax.ShapeDtypeStruct(kept.shape, BF16),
        compiler_params=ROOM,
    )(kept, arrived, slope)


def weight_kernel(own_picked, mate_picked, own_pre, mate_pre, *out_refs):
    share = out_refs[0].shape[0]
    picked = jnp.concatenate([own_picked[...], mate_picked[...]], axis=0)
    pre = jnp.concatenate([own_pre[...], mate_pre[...]], axis=0)
    product = dot_of(picked, pre, 0, 0)
    for d, out_ref in enumerate(out_refs):
        out_ref[...] = product[d * share : (d + 1) * share].astype(out_ref.dtype)


def weight_parts(own_picked, mate_picked, own_pre, mate_pre, count):
    half, features = own_picked.shape[1], own_pre.shape[1]
    shape = (half // count, features)
    return pl.pallas_call(
        weight_kernel,
        out_shape=[jax.ShapeDtypeStruct(shape, F32 if d == 0 else BF16) for d in range(count)],
        compiler_params=ROOM,
    )(own_picked, mate_picked, own_pre, mate_pre)


def shards(audio, video, owner, clip_feats, lengths, proj_weight):
    clips, features = audio.shape
    blocks = lax.axis_size(BLK)
    core = lax.axis_index("wide_c")
    place = lax.axis_index("blk_z").astype(jnp.int32)[None]
    audio_line = lax.all_gather(audio, "blk_z", axis=0, tiled=True)

    peers = lax.axis_size(WIDE)
    slots = clip_feats.shape[0]
    capacity = slots // peers
    length_scale = lax.rsqrt(lengths.astype(F32))[:, None]
    pooled = (clip_feats.astype(F32) * length_scale).astype(BF16)
    pooled_slots = lax.all_to_all(
        pooled.reshape(peers, capacity, features), WIDE, 0, 0, tiled=True
    ).reshape(slots, features)
    video_mate = swapped(video, "blk_x")
    slope_own = gelu_slope(dot_of(pooled, proj_weight, 1, 0))

    targets = targets_of(owner, capacity)
    placing = (targets[:, None] == jnp.arange(slots, dtype=jnp.int32)[None, :]).astype(BF16)
    clip_rows = dot_of(placing, pooled_slots, 1, 0).astype(BF16)
    slope_rows = gelu_slope(dot_of(clip_rows, proj_weight, 1, 0))
    picked = dot_of(clip_rows, picking_of(core, features), 1, 0).astype(BF16)
    picked_mate = swapped(
        dot_of(clip_rows, picking_of(1 - core, features), 1, 0).astype(BF16), "wide_c"
    )
    audio_line, video_mate, slope_rows, picked, picked_mate, slope_own, targets = (
        lax.optimization_barrier(
            (audio_line, video_mate, slope_rows, picked, picked_mate, slope_own, targets)
        )
    )

    kept, sent, line_grads = pair_grads(audio_line, video, video_mate, place, 4.0 / blocks, 4)
    audio_grad = lax.psum_scatter(line_grads, "blk_z", scatter_dimension=0, tiled=True)
    arrived = swapped(sent, "blk_x")
    packed = clip_grads(kept, arrived, targets, slots)
    pre_rows = product_rows(kept, arrived, slope_rows)
    received = lax.all_to_all(
        packed.reshape(peers, capacity, features), WIDE, 0, 0, tiled=True
    ).reshape(slots, features)

    pre_mate = swapped(pre_rows, "wide_c")
    keep, give = weight_parts(picked, picked_mate, pre_rows, pre_mate, 2)
    summed = (keep + swapped(give, "blk_x").astype(F32)).astype(BF16)
    summed, received = lax.optimization_barrier((summed, received))
    chips = peers // 2
    pieces = lax.all_to_all(
        summed.reshape(chips, -1, features), ("wide_y", "wide_x"), 0, 0, tiled=True
    )
    pre_grad = (received.astype(F32) * slope_own).astype(BF16)
    feats_grad = (dot_of(pre_grad, proj_weight, 1, 1) * length_scale).astype(BF16)
    pieces, feats_grad = lax.optimization_barrier((pieces, feats_grad))
    total = jnp.sum(pieces.astype(F32), axis=0).astype(BF16)
    gathered = lax.all_to_all(
        jnp.broadcast_to(total[None], (blocks, *total.shape)), BLK, 0, 0, tiled=True
    )
    gathered = gathered.reshape(lax.axis_size("blk_x"), -1, *total.shape)
    weight_grad = jnp.sum(gathered.astype(F32), axis=1).reshape(-1, features)
    return (audio_grad, feats_grad, weight_grad)


def solution(mesh):
    finer = Mesh(mesh.devices.reshape(8, 2, 2, 2, 8), AXES)
    rows = P(AXES, None)
    return jax.shard_map(
        shards,
        mesh=finer,
        in_specs=(rows, rows, rows, rows, P(AXES), P()),
        out_specs=(rows, rows, P(WIDE, None)),
        check_vma=False,
    )
```

```python
import jax
import jax.numpy as jnp
from jax import lax
from jax.experimental import pallas as pl
from jax.experimental.pallas import tpu as pltpu
from jax.sharding import Mesh
from jax.sharding import PartitionSpec as P

AXES = ("wide_y", "wide_x", "wide_c", "blk_x", "blk_z")
WIDE = ("wide_y", "wide_x", "wide_c")
BLK = ("blk_x", "blk_z")
BF16 = jnp.bfloat16
F32 = jnp.float32
ROOM = pltpu.CompilerParams(vmem_limit_bytes=24 * 2**20)
ALL_ROOM = pltpu.CompilerParams(vmem_limit_bytes=56 * 2**20)
SCALAR = pl.BlockSpec(memory_space=pltpu.SMEM)


def swapped(array, axis):
    return lax.ppermute(array, axis, [(0, 1), (1, 0)])


def dot_of(matrix_a, matrix_b, dim_a, dim_b):
    return lax.dot_general(
        matrix_a, matrix_b, (((dim_a,), (dim_b,)), ((), ())), preferred_element_type=F32
    )


def gelu_slope(v):
    cdf = 0.5 * (1.0 + lax.erf(v * 0.7071067811865476))
    return cdf + v * (0.3989422804014327 * jnp.exp(-0.5 * v * v))


def targets_of(owner, capacity):
    ids = jnp.arange(owner.shape[0], dtype=jnp.int32)
    peer = owner[:, 0]
    before = (peer[:, None] == peer[None, :]) & (ids[:, None] < ids[None, :])
    return peer * capacity + jnp.sum(before.astype(jnp.int32), axis=0)


def picking_of(core, feature_count):
    half = feature_count // 2
    ny, nx = lax.axis_size("wide_y"), lax.axis_size("wide_x")
    bx = lax.axis_size("blk_x")
    share = half // (ny * nx * bx)
    place = jnp.arange(half, dtype=jnp.int32)
    within, rest = place % share, place // share
    y, apart = rest % ny, rest // ny
    x_wide = (apart // bx) ^ lax.axis_index("wide_x")
    x_blk = (apart % bx) ^ lax.axis_index("blk_x")
    feature = (((y * nx + x_wide) * 2 + core) * bx + x_blk) * share + within
    return (jnp.arange(feature_count, dtype=jnp.int32)[:, None] == feature[None, :]).astype(BF16)


def pair_kernel(factor, steps, place_ref, line_hbm, own_hbm, mate_hbm,
                kept_ref, sent_ref, grads_hbm, line, video, grads, total, came, gone):
    rows, clips = line.shape[0] // steps, own_hbm.shape[0]
    loads = [
        pltpu.make_async_copy(own_hbm, video.at[pl.ds(0, clips)], came.at[0]),
        pltpu.make_async_copy(mate_hbm, video.at[pl.ds(clips, clips)], came.at[1]),
    ]
    for step in range(steps):
        block = pl.ds(step * rows, rows)
        loads.append(pltpu.make_async_copy(line_hbm.at[block], line.at[block], came.at[2 + step]))
    for load in loads:
        load.start()
    loads[0].wait()
    loads[1].wait()

    def coeffs_of(step):
        block = pl.ds(step * rows, rows)
        loads[2 + step].wait()
        scores = dot_of(video[...], line[block], 1, 1)
        row = lax.broadcasted_iota(jnp.int32, scores.shape, 0)
        col = lax.broadcasted_iota(jnp.int32, scores.shape, 1) + step * rows
        labels = ((col == place_ref[0] * clips + row) & (row < clips)).astype(F32)
        return (factor * (jax.nn.sigmoid(4.0 * scores - 2.0) - labels)).astype(BF16)

    stores = []
    coeffs = coeffs_of(0)
    for step in range(steps):
        block = pl.ds(step * rows, rows)
        ready = coeffs
        if step + 1 < steps:
            coeffs = coeffs_of(step + 1)
        part = dot_of(ready, line[block], 1, 0)
        if step == 0:
            total[...] = part
        else:
            total[...] += part
        grads[block] = dot_of(ready, video[...], 0, 0).astype(BF16)
        stores.append(pltpu.make_async_copy(grads.at[block], grads_hbm.at[block], gone.at[step]))
        stores[-1].start()
    kept_ref[...] = total[:clips]
    sent_ref[...] = total[clips:].astype(BF16)
    for store in stores:
        store.wait()


def pair_grads(line, own, mate, place, factor, steps):
    rows, features = line.shape
    clips = own.shape[0]
    free = pl.BlockSpec(memory_space=pl.ANY)
    held = pl.BlockSpec(memory_space=pltpu.VMEM)
    return pl.pallas_call(
        lambda *refs: pair_kernel(factor, steps, *refs),
        in_specs=[SCALAR, free, free, free],
        out_specs=[held, held, free],
        out_shape=[
            jax.ShapeDtypeStruct((clips, features), F32),
            jax.ShapeDtypeStruct((clips, features), BF16),
            jax.ShapeDtypeStruct((rows, features), BF16),
        ],
        scratch_shapes=[
            pltpu.VMEM((rows, features), BF16),
            pltpu.VMEM((2 * clips, features), BF16),
            pltpu.VMEM((rows, features), BF16),
            pltpu.VMEM((2 * clips, features), F32),
            pltpu.SemaphoreType.DMA((2 + steps,)),
            pltpu.SemaphoreType.DMA((steps,)),
        ],
        compiler_params=ALL_ROOM,
        cost_estimate=pl.CostEstimate(
            flops=12 * rows * clips * features, bytes_accessed=5 * rows * features, transcendentals=0
        ),
    )(place, line, own, mate)


def clip_kernel(kept_ref, arrived_ref, target_ref, packed_ref):
    grad = (kept_ref[...] + arrived_ref[...].astype(F32)).astype(BF16)
    slots, clips = packed_ref.shape[0], grad.shape[0]
    slot = lax.broadcasted_iota(jnp.int32, (slots, clips), 0)
    placing = (slot == target_ref[...]).astype(BF16)
    packed_ref[...] = dot_of(placing, grad, 1, 0).astype(BF16)


def clip_grads(kept, arrived, targets, slots):
    return pl.pallas_call(
        clip_kernel,
        out_shape=jax.ShapeDtypeStruct((slots, kept.shape[1]), BF16),
        compiler_params=ROOM,
    )(kept, arrived, targets[None, :])


def product_kernel(kept_ref, arrived_ref, slope_ref, pre_ref):
    grad = (kept_ref[...] + arrived_ref[...].astype(F32)).astype(BF16)
    pre_ref[...] = (grad.astype(F32) * slope_ref[...]).astype(BF16)


def product_rows(kept, arrived, slope):
    return pl.pallas_call(
        product_kernel,
        out_shape=jax.ShapeDtypeStruct(kept.shape, BF16),
        compiler_params=ROOM,
    )(kept, arrived, slope)


def weight_kernel(own_picked, mate_picked, own_pre, mate_pre, *out_refs):
    share = out_refs[0].shape[0]
    picked = jnp.concatenate([own_picked[...], mate_picked[...]], axis=0)
    pre = jnp.concatenate([own_pre[...], mate_pre[...]], axis=0)
    product = dot_of(picked, pre, 0, 0)
    for d, out_ref in enumerate(out_refs):
        out_ref[...] = product[d * share : (d + 1) * share].astype(out_ref.dtype)


def weight_parts(own_picked, mate_picked, own_pre, mate_pre, count):
    half, features = own_picked.shape[1], own_pre.shape[1]
    shape = (half // count, features)
    return pl.pallas_call(
        weight_kernel,
        out_shape=[jax.ShapeDtypeStruct(shape, F32 if d == 0 else BF16) for d in range(count)],
        compiler_params=ROOM,
    )(own_picked, mate_picked, own_pre, mate_pre)


def shards(audio, video, owner, clip_feats, lengths, proj_weight):
    clips, features = audio.shape
    blocks = lax.axis_size(BLK)
    core = lax.axis_index("wide_c")
    place = lax.axis_index("blk_z").astype(jnp.int32)[None]
    audio_line = lax.all_gather(audio, "blk_z", axis=0, tiled=True)

    peers = lax.axis_size(WIDE)
    slots = clip_feats.shape[0]
    capacity = slots // peers
    length_scale = lax.rsqrt(lengths.astype(F32))[:, None]
    pooled = (clip_feats.astype(F32) * length_scale).astype(BF16)
    pooled_slots = lax.all_to_all(
        pooled.reshape(peers, capacity, features), WIDE, 0, 0, tiled=True
    ).reshape(slots, features)
    video_mate = swapped(video, "blk_x")
    slope_own = gelu_slope(dot_of(pooled, proj_weight, 1, 0))

    targets = targets_of(owner, capacity)
    placing = (targets[:, None] == jnp.arange(slots, dtype=jnp.int32)[None, :]).astype(BF16)
    clip_rows = dot_of(placing, pooled_slots, 1, 0).astype(BF16)
    slope_rows = gelu_slope(dot_of(clip_rows, proj_weight, 1, 0))
    picked = dot_of(clip_rows, picking_of(core, features), 1, 0).astype(BF16)
    picked_mate = swapped(
        dot_of(clip_rows, picking_of(1 - core, features), 1, 0).astype(BF16), "wide_c"
    )
    audio_line, video_mate, slope_rows, picked, picked_mate, slope_own, targets = (
        lax.optimization_barrier(
            (audio_line, video_mate, slope_rows, picked, picked_mate, slope_own, targets)
        )
    )

    kept, sent, line_grads = pair_grads(audio_line, video, video_mate, place, 4.0 / blocks, 4)
    audio_grad = lax.psum_scatter(line_grads, "blk_z", scatter_dimension=0, tiled=True)
    arrived = swapped(sent, "blk_x")
    packed = clip_grads(kept, arrived, targets, slots)
    pre_rows = product_rows(kept, arrived, slope_rows)
    received = lax.all_to_all(
        packed.reshape(peers, capacity, features), WIDE, 0, 0, tiled=True
    ).reshape(slots, features)

    pre_mate = swapped(pre_rows, "wide_c")
    parts = weight_parts(picked, picked_mate, pre_rows, pre_mate, 4)
    summed = parts[0]
    for d in (1, 3, 2):
        pairs = [(at, at ^ d) for at in range(4)]
        summed = summed + lax.ppermute(parts[d], ("wide_x", "blk_x"), pairs).astype(F32)
    summed = summed.astype(BF16)
    summed, received = lax.optimization_barrier((summed, received))
    ny = lax.axis_size("wide_y")
    pieces = lax.all_to_all(summed.reshape(ny, -1, features), "wide_y", 0, 0, tiled=True)
    pre_grad = (received.astype(F32) * slope_own).astype(BF16)
    feats_grad = (dot_of(pre_grad, proj_weight, 1, 1) * length_scale).astype(BF16)
    pieces, feats_grad = lax.optimization_barrier((pieces, feats_grad))
    total = jnp.sum(pieces.astype(F32), axis=0).astype(BF16)
    gathered = lax.all_to_all(
        jnp.broadcast_to(total[None], (blocks, *total.shape)), BLK, 0, 0, tiled=True
    )
    gathered = gathered.reshape(lax.axis_size("blk_x"), -1, *total.shape)
    weight_grad = jnp.sum(gathered.astype(F32), axis=1).reshape(-1, features)
    return (audio_grad, feats_grad, weight_grad)


def solution(mesh):
    finer = Mesh(mesh.devices.reshape(8, 2, 2, 2, 8), AXES)
    rows = P(AXES, None)
    return jax.shard_map(
        shards,
        mesh=finer,
        in_specs=(rows, rows, rows, rows, P(AXES), P()),
        out_specs=(rows, rows, P(WIDE, None)),
        check_vma=False,
    )
```
